32 devices in a mesh: gx: 4 (over z), gy: 8 (over y, x, core).
Axes of the slice: x: 2, y: 2, z: 4, core: 2. Of those that a mesh axis runs over, the one named last changes fastest.
Arguments:
- gaseous_rho: float32 [16, 768, 512], P(None, 'gy', 'gx'), may hold values from 0.5 to 2
- gaseous_flow_vector: float32 [3, 16, 768, 512], P(None, None, 'gy', 'gx'), may hold values from -1 to 1
- gaseous_kelvin: float32 [16, 768, 512], P(None, 'gy', 'gx'), may hold values from 0.5 to 2
- sender_tile_map: int32 [32, 256], P(('gx', 'gy')), may hold values from -1 to 1535, as said below
- receiver_arrival_rank: int32 [2048], P(('gx', 'gy')), may hold values from -1 to 255, as said below
- bin_active_number: int32 [2048], P(('gx', 'gy')), may hold values from 0 to 512, as said below
- grain_inertia: float32 [2048, 512], P(('gx', 'gy')), may hold values from 0.05 to 0.5
- grain_motion_vector: float32 [3, 2048, 512], P(None, ('gx', 'gy')), may hold values from -5 to 5
- grain_kelvin: float32 [2048, 512], P(('gx', 'gy')), may hold values from 0.5 to 4
- grain_voxel_number: int32 [2048, 512], P(('gx', 'gy')), may hold values from 0 to 127
- grain_substance_label: int32 [2048, 512], P(('gx', 'gy')), may hold values from 0 to 1
- exchange_factor: float32 [2, 2], replicated, may hold values from 0.5 to 4
Outputs:
- gas_state_out: float32 [5, 16, 768, 512], P(None, None, 'gy', 'gx')
- solid_state: float32 [4, 2048, 2, 128], P(None, ('gx', 'gy'))
The draws below stay inside these ranges and needn't reach their ends.
Inputs may be any that keep to these rules, and one draw needn't show every extreme that they name: sender_tile_map[s, o * 8 + r] is the local block that device s sends as its r-th block to owner o, -1 where it sends fewer; the blocks of one device are distinct; only 8 devices send, each to every owner. `receiver_arrival_rank`: an owner's live slots come first, 48 or more of them, and name each sent block of that owner once; in each draw some owner has all 64 live and receives exactly 8 blocks from each sending device. `bin_active_number`: 0 exactly on slots with receiver_arrival_rank -1, else 512 // 2 or more; some slot holds 512.
All inputs are finite; a program needn't handle non-finite values.
Results may differ from the reference program's by a relative error of at most 0.0003.
Values sent between devices are 32-bit elements; how exact they have to be, the bound alone decides.
A program may use at most 128 MiB of HBM per device.

```python
import math
import jax
import jax.numpy as jnp
from jax import lax

CX = 128
CY = 96
CZ = 16
SLOTS = 64
BIN_CAPACITY = 512
CAP = 8
GRID_WIDTH_EAST = 512
GRID_WIDTH_NORTH = 768
GRID_WIDTH_UPWARD = 16
RECEIVER_BINS = 2048
N_GX = 4
N_GY = 8


def first_last(order, length):
    positions = jnp.arange(length)
    last = length - 1
    return jnp.where(positions == 0, last, jnp.where(order == last, order[0], order))


def shuffle(subkey):
    return first_last(jax.random.permutation(subkey, CZ * CY), CZ * CY)


def routing(key):
    devices = N_GX * N_GY
    hot_count = devices // 4
    capacity = 4 * SLOTS // devices
    subkeys = jax.random.split(key, 6)
    filled = jax.random.randint(subkeys[0], (devices,), 3 * SLOTS // 4, SLOTS + 1)
    fullest = jax.random.randint(subkeys[1], (), 0, devices)
    filled = filled.at[(fullest + 1) % devices].set(3 * SLOTS // 4)
    filled = filled.at[fullest].set(SLOTS)
    offset = jax.random.randint(subkeys[2], (devices,), 0, hot_count)
    hot_devices = first_last(jax.random.permutation(subkeys[3], devices), devices)[:hot_count]
    position = jnp.arange(SLOTS)[None, :]
    present = position < filled[:, None]
    source = hot_devices[(position + offset[:, None]) % hot_count]
    queue_rank = position // hot_count
    receiver_arrival_rank = jnp.where(present, source * capacity + queue_rank, -1)
    orders = jax.vmap(shuffle)(jax.random.split(subkeys[4], devices))
    owner_index = jnp.arange(devices)[:, None]
    column = owner_index * capacity + queue_rank
    chosen = orders[source, column].astype(jnp.int32)
    send_rows = jnp.full((devices, devices * capacity), -1, jnp.int32)
    send_rows = send_rows.at[jnp.where(present, source, devices), column].set(chosen, mode='drop')
    counts = jax.random.randint(subkeys[5], (devices, SLOTS), BIN_CAPACITY // 2, BIN_CAPACITY + 1)
    counts = counts.at[fullest, 0].set(BIN_CAPACITY)
    counts = jnp.where(present, counts, 0)
    return (send_rows, receiver_arrival_rank.reshape(-1).astype(jnp.int32), counts.reshape(-1).astype(jnp.int32))


def draw_sender_tile_map(key, part):
    return routing(key)[0]


def draw_receiver_arrival_rank(key, part):
    return routing(key)[1]


def draw_bin_active_number(key, part):
    return routing(key)[2]


def with_ends(result, key, smallest, high):
    dims = result.shape
    spot = [jax.random.randint(jax.random.fold_in(key, axis), (), 0, dims[axis]) for axis in range(len(dims))]
    result = result.at[tuple(spot)].set(smallest)
    longest = dims.index(max(dims))
    spot[longest] = (spot[longest] + 1) % dims[longest]
    return result.at[tuple(spot)].set(high)


def block_scale(own_key, extent, cuts, smallest, high):
    def one(dim, parts):
        draws = jax.random.uniform(jax.random.fold_in(jax.random.fold_in(own_key, 6), dim), (parts,), jnp.float32, smallest / len(cuts), high / len(cuts))
        return jnp.repeat(jnp.exp(draws), extent[dim] // parts).reshape((-1,) + (1,) * (len(extent) - dim - 1))

    loudness = one(*cuts[0])
    for cut in cuts[1:]:
        loudness = loudness * one(*cut)
    return loudness


def centred(stream_key, shape, deviation, bound, cuts=(), dtype=jnp.bfloat16):
    result = deviation * jax.random.normal(stream_key, shape, jnp.float32)
    if cuts:
        result = result * block_scale(stream_key, shape, cuts, -0.22, 0.18)
    return jnp.clip(result, -bound, bound).astype(dtype)


def setup_inputs(seed: int = 0) -> dict:
    arg_keys = jax.random.split(jax.random.key(seed), 13)
    gaseous_rho = jnp.clip(0.5 + 1.5 * jax.random.uniform(arg_keys[0], (GRID_WIDTH_UPWARD, GRID_WIDTH_NORTH, GRID_WIDTH_EAST), jnp.float32) ** block_scale(arg_keys[0], (GRID_WIDTH_UPWARD, GRID_WIDTH_NORTH, GRID_WIDTH_EAST), ((1, 8), (2, 4)), -0.2, 0.2), 0.5, 2.0)
    gaseous_flow_vector = jnp.clip(jax.random.uniform(arg_keys[1], (3, GRID_WIDTH_UPWARD, GRID_WIDTH_NORTH, GRID_WIDTH_EAST), jnp.float32, -1.0, 1.0) * block_scale(arg_keys[1], (3, GRID_WIDTH_UPWARD, GRID_WIDTH_NORTH, GRID_WIDTH_EAST), ((2, 8), (3, 4)), -0.4, 0.0), -1.0, 1.0)
    gaseous_kelvin = jnp.clip(0.5 + 1.5 * jax.random.uniform(arg_keys[2], (GRID_WIDTH_UPWARD, GRID_WIDTH_NORTH, GRID_WIDTH_EAST), jnp.float32) ** block_scale(arg_keys[2], (GRID_WIDTH_UPWARD, GRID_WIDTH_NORTH, GRID_WIDTH_EAST), ((1, 8), (2, 4)), -0.2, 0.2), 0.5, 2.0)
    sender_tile_map = draw_sender_tile_map(jax.random.fold_in(arg_keys[12], 71), 0)
    receiver_arrival_rank = draw_receiver_arrival_rank(jax.random.fold_in(arg_keys[12], 71), 0)
    bin_active_number = draw_bin_active_number(jax.random.fold_in(arg_keys[12], 71), 0)
    grain_inertia = jnp.clip(jnp.exp(math.log(0.5) - 2.3025851 * jax.random.uniform(arg_keys[6], (RECEIVER_BINS, BIN_CAPACITY), jnp.float32) ** block_scale(arg_keys[6], (RECEIVER_BINS, BIN_CAPACITY), ((0, 32),), -0.2, 0.2)), 0.05, 0.5)
    grain_motion_vector = centred(arg_keys[7], (3, RECEIVER_BINS, BIN_CAPACITY), 1.0, 5.0, ((1, 32),), jnp.float32)
    grain_kelvin = jnp.clip(0.5 + 3.5 * jax.random.uniform(arg_keys[8], (RECEIVER_BINS, BIN_CAPACITY), jnp.float32) ** block_scale(arg_keys[8], (RECEIVER_BINS, BIN_CAPACITY), ((0, 32),), -0.2, 0.2), 0.5, 4.0)
    grain_voxel_number = with_ends(jax.random.randint(arg_keys[9], (RECEIVER_BINS, BIN_CAPACITY), 0, CX), jax.random.fold_in(arg_keys[9], 1), 0, CX - 1).astype(jnp.int32)
    grain_substance_label = with_ends(jax.random.randint(arg_keys[10], (RECEIVER_BINS, BIN_CAPACITY), 0, 2), jax.random.fold_in(arg_keys[10], 1), 0, 1).astype(jnp.int32)
    exchange_factor = jnp.clip(jnp.exp(jax.random.uniform(arg_keys[11], (2, 2), jnp.float32, math.log(0.5), math.log(4.0))), 0.5, 4.0)
    return dict(gaseous_rho=gaseous_rho, gaseous_flow_vector=gaseous_flow_vector, gaseous_kelvin=gaseous_kelvin, sender_tile_map=sender_tile_map, receiver_arrival_rank=receiver_arrival_rank, bin_active_number=bin_active_number, grain_inertia=grain_inertia, grain_motion_vector=grain_motion_vector, grain_kelvin=grain_kelvin, grain_voxel_number=grain_voxel_number, grain_substance_label=grain_substance_label, exchange_factor=exchange_factor)


step_ratio = 0.08


def edge_mask(length):
    positions = jnp.arange(length + 1)
    return (positions == 0) | (positions == length)


def face_pair(quantity_array, direction):
    ndims = quantity_array.ndim
    lower_index = [slice(None)] * (ndims - 3) + [slice(1, -1)] * 3
    upper_index = list(lower_index)
    lower_index[ndims - 3 + direction] = slice(0, -1)
    upper_index[ndims - 3 + direction] = slice(1, None)
    return quantity_array[tuple(lower_index)], quantity_array[tuple(upper_index)]


def advance(padded, wall_masks):
    density = padded[0]
    pressure = padded[0] * padded[4]
    conserved = jnp.concatenate([padded[0:1], padded[0:1] * padded[1:4], padded[0:1] * padded[4:5]], 0)
    change = 0.0
    for direction in range(3):
        dens_lower, dens_upper = face_pair(density, direction)
        press_lower, press_upper = face_pair(pressure, direction)
        normal_lower, normal_upper = face_pair(padded[3 - direction], direction)
        face_speed = 0.5 * (normal_lower + normal_upper) - step_ratio * (press_upper - press_lower) * 2.0 / (dens_lower + dens_upper)
        mask_shape = [1, 1, 1]
        mask_shape[direction] = -1
        face_speed = jnp.where(wall_masks[direction].reshape(mask_shape), 0.0, face_speed)
        cons_lower, cons_upper = face_pair(conserved, direction)
        face_flux = face_speed * jnp.where(face_speed > 0, cons_lower, cons_upper)
        count_faces = face_flux.shape[1 + direction]
        change = change + lax.slice_in_dim(face_flux, 1, count_faces, axis=1 + direction) - lax.slice_in_dim(face_flux, 0, count_faces - 1, axis=1 + direction)
    central = conserved[:, 1:-1, 1:-1, 1:-1]
    updated = central - step_ratio * change
    return jnp.concatenate([updated[0:1], updated[1:4] / updated[0:1], updated[4:5] / updated[0:1]], 0)


def grain_quantities(grain_inertia, grain_motion_vector, grain_kelvin, bin_active_number):
    padding = grain_inertia.shape[1]
    present = jnp.arange(padding)[None, :] < bin_active_number[:, None]
    inertia_scaled = jnp.where(present, grain_inertia, 0.0)
    return jnp.stack([inertia_scaled, inertia_scaled * grain_motion_vector[0], inertia_scaled * grain_motion_vector[1], inertia_scaled * grain_motion_vector[2], inertia_scaled * grain_kelvin], 0)


def couple(gas, grid, exchange_factor):
    gaseous_inertia = gas[0]
    gaseous_motion = gas[1:4]
    gaseous_enthalpy = gas[4]
    rigid_inertia = grid[0]
    solid_momentum = grid[1:4]
    rigid_enthalpy = grid[4]
    drag = exchange_factor[:, 0][None, :, None]
    thermal_coupler = exchange_factor[:, 1][None, :, None]
    drag_total = rigid_inertia + drag
    next_flow_vector = (gaseous_inertia * gaseous_motion + jnp.sum(drag * solid_momentum / drag_total, axis=2)) / (gaseous_inertia + jnp.sum(drag * rigid_inertia / drag_total, axis=1))
    rigid_motion_vector = (solid_momentum + drag * next_flow_vector[:, :, None, :]) / drag_total
    summed_enthalpy = rigid_inertia + thermal_coupler
    next_kelvin = (gaseous_inertia * gaseous_enthalpy + jnp.sum(thermal_coupler * rigid_enthalpy / summed_enthalpy, axis=1)) / (gaseous_inertia + jnp.sum(thermal_coupler * rigid_inertia / summed_enthalpy, axis=1))
    rigid_kelvin = (rigid_enthalpy + thermal_coupler * next_kelvin[:, None, :]) / summed_enthalpy
    increment_changes = jnp.concatenate([next_flow_vector - gaseous_motion, (next_kelvin - gaseous_enthalpy)[None]], 0)
    rigid_constituent = jnp.concatenate([rigid_motion_vector, rigid_kelvin[None]], 0)
    return increment_changes, rigid_constituent


def reference(gaseous_rho, gaseous_flow_vector, gaseous_kelvin, sender_tile_map, receiver_arrival_rank, bin_active_number, grain_inertia, grain_motion_vector, grain_kelvin, grain_voxel_number, grain_substance_label, exchange_factor):
    voxel_record = jnp.concatenate([gaseous_rho[None], gaseous_flow_vector, gaseous_kelvin[None]], 0)
    padded = jnp.pad(voxel_record, ((0, 0), (1, 1), (1, 1), (1, 1)))
    advanced = advance(padded, [edge_mask(GRID_WIDTH_UPWARD), edge_mask(GRID_WIDTH_NORTH), edge_mask(GRID_WIDTH_EAST)])
    devices = N_GX * N_GY
    blocks = advanced.reshape(5, GRID_WIDTH_UPWARD, N_GY, CY, N_GX, CX).transpose(0, 4, 2, 1, 3, 5).reshape(5, devices, GRID_WIDTH_UPWARD * CY, CX)
    slot_owner = jnp.arange(RECEIVER_BINS) // SLOTS
    live_slot = receiver_arrival_rank >= 0
    safe_source = jnp.maximum(receiver_arrival_rank, 0)
    source_device = safe_source // CAP
    source_rank = safe_source % CAP
    local_block = sender_tile_map[source_device, slot_owner * CAP + source_rank]
    gas = blocks[:, source_device, local_block]
    quantity_array = grain_quantities(grain_inertia, grain_motion_vector, grain_kelvin, bin_active_number)
    target = (jnp.arange(RECEIVER_BINS)[:, None] * 2 + grain_substance_label) * CX + grain_voxel_number
    summed = jax.ops.segment_sum(quantity_array.reshape(5, -1).T, target.reshape(-1), num_segments=RECEIVER_BINS * 2 * CX)
    grid = summed.T.reshape(5, RECEIVER_BINS, 2, CX)
    increment_changes, rigid_constituent = couple(gas, grid, exchange_factor)
    target_device = jnp.where(live_slot, source_device, devices)
    gains = jnp.zeros_like(blocks[1:]).at[:, target_device, local_block].add(increment_changes, mode="drop")
    final = jnp.concatenate([blocks[0:1], blocks[1:] + gains], 0)
    gas_state_out = final.reshape(5, N_GX, N_GY, GRID_WIDTH_UPWARD, CY, CX).transpose(0, 3, 2, 4, 1, 5).reshape(5, GRID_WIDTH_UPWARD, GRID_WIDTH_NORTH, GRID_WIDTH_EAST)
    solid_state = jnp.where(live_slot[None, :, None, None], rigid_constituent, 0.0)
    return gas_state_out, solid_state
```

```python
import functools

import jax
import jax.numpy as jnp
from jax import lax
from jax.experimental import pallas as pl
from jax.experimental.pallas import tpu as pltpu
from jax.sharding import PartitionSpec as P

MESH = pl.DeviceIdType.MESH
VMEM = pl.BlockSpec(memory_space=pltpu.VMEM)
SMEM = pl.BlockSpec(memory_space=pltpu.SMEM)
step_ratio = 0.08
limit = 56 * 1024 * 1024
sent = 6
back = 4


def coefficients(ex_ref, m):
    rows = lax.broadcasted_iota(jnp.int32, (8, 128), 0)
    return jnp.where(rows < 4, ex_ref[m, 0], ex_ref[m, 1])


def bin_kernel(
    cap, rank_ref, count_ref, ex_ref, mass_ref, vel_ref, temp_ref, vox_ref, lab_ref, pay_ref, sums_ref
):
    slots, padding = mass_ref.shape
    width = pay_ref.shape[2]
    pay_ref[...] = jnp.zeros_like(pay_ref)
    rows = lax.broadcasted_iota(jnp.int32, (8, padding), 0)
    lane = lax.broadcasted_iota(jnp.int32, (1, padding), 1)
    cells = lax.broadcasted_iota(jnp.int32, (width, padding), 0)
    factor = [coefficients(ex_ref, m) for m in range(2)]
    unroll = 4

    def body(i, carry):
        for u in range(unroll):
            k = i * unroll + u
            here = pl.ds(k, 1)
            mass = jnp.where(lane < count_ref[k], mass_ref[here, :], 0.0)
            base = jnp.where(rows == 4, temp_ref[here, :], 1.0)
            for c in range(3):
                base = jnp.where(rows == c + 1, vel_ref[c, here, :], base)
            base = base * mass
            label = lab_ref[here, :]
            values = jnp.concatenate(
                [jnp.where(label == 0, base, 0.0), jnp.where(label == 1, base, 0.0)], 0
            )
            high = values.astype(jnp.bfloat16)
            low = (values - high.astype(jnp.float32)).astype(jnp.bfloat16)
            onehot = jnp.where(cells == vox_ref[here, :], 1.0, 0.0).astype(jnp.bfloat16)
            total = lax.dot_general(
                jnp.concatenate([high, low], 0),
                onehot,
                (((1,), (1,)), ((), ())),
                preferred_element_type=jnp.float32,
            )
            total = total[:16] + total[16:]
            sums_ref[k] = total
            pay = 0.0
            for m in range(2):
                part = total[8 * m : 8 * m + 8]
                pay = pay + factor[m] * part / (part[0:1] + factor[m])
            v = rank_ref[k]

            @pl.when(v >= 0)
            def _():
                s = v // cap
                r = v % cap
                for j in range(sent):
                    pay_ref[s, pl.ds(j * cap + r, 1), :] = pay[j : j + 1]

        return carry

    lax.fori_loop(0, slots // unroll, body, 0)


def face(a, b, ua, ub, wall):
    speed = 0.5 * (ua + ub) - (2.0 * step_ratio) * (b[4] - a[4]) / (a[0] + b[0])
    speed = jnp.where(wall, 0.0, speed)
    ahead = speed > 0
    return [speed * jnp.where(ahead, x, y) for x, y in zip(a, b)]


def conserve(prim):
    rho = prim[0]
    return [rho] + [rho * q for q in prim[1:]]


def grid_kernel(
    n_gx,
    n_gy,
    map_ref,
    rho_ref,
    vel_ref,
    temp_ref,
    pay_ref,
    adv_ref,
    new_ref,
    ret_ref,
    xsend,
    xrecv,
    ysend,
    yrecv,
    got,
    home,
    ext,
    flux_z,
    picked,
    halo_send,
    halo_recv,
    pay_send,
    pay_recv,
    back_send,
    back_recv,
):
    n = n_gx * n_gy
    depth, height, width = rho_ref.shape
    cap = map_ref.shape[1] // n
    gx = lax.axis_index("gx")
    gy = lax.axis_index("gy")
    me = gx * n_gy + gy

    def place(d):
        return (d // n_gy, lax.rem(d, n_gy))

    barrier = pltpu.get_barrier_semaphore()

    def greet(k, carry):
        d = lax.rem(me + k, n)
        pl.semaphore_signal(barrier, inc=1, device_id=place(d), device_id_type=MESH)
        return carry

    lax.fori_loop(1, n, greet, 0)

    def prim(f, z, rows):
        if f == 0:
            return rho_ref[z, rows, :]
        if f == 4:
            return temp_ref[z, rows, :]
        return vel_ref[f - 1, z, rows, :]

    whole = pl.ds(0, height)
    lanes = lax.broadcasted_iota(jnp.int32, (height, width), 1)

    def pack(z, carry):
        low, high = carry
        for f in range(5):
            spot = f * depth + z
            x = prim(f, z, whole)
            ysend[0, f, pl.ds(z, 1), :] = x[0:1]
            ysend[1, f, pl.ds(z, 1), :] = x[height - 1 : height]
            low = jnp.where(lanes == spot, pltpu.roll(x, spot, 1), low)
            high = jnp.where(lanes == spot, pltpu.roll(x, spot + 1, 1), high)
        return (low, high)

    zero = jnp.zeros((height, width), jnp.float32)
    low, high = lax.fori_loop(0, depth, pack, (zero, zero))
    xsend[0] = low
    xsend[1] = high
    pl.semaphore_wait(barrier, n - 1)

    def halo(which, side, device):
        src, dst = ((xsend, xrecv), (ysend, yrecv))[which]
        return pltpu.make_async_remote_copy(
            src_ref=src.at[side],
            dst_ref=dst.at[1 - side],
            send_sem=halo_send.at[2 * which + side],
            recv_sem=halo_recv.at[2 * which + 1 - side],
            device_id=device,
            device_id_type=MESH,
        )

    sides = (
        (0, 0, gx > 0, (gx - 1, gy)),
        (0, 1, gx < n_gx - 1, (gx + 1, gy)),
        (1, 0, gy > 0, (gx, gy - 1)),
        (1, 1, gy < n_gy - 1, (gx, gy + 1)),
    )
    for which, side, there, device in sides:

        @pl.when(there)
        def _(which=which, side=side, device=device):
            halo(which, side, device).start()

    def outward(k):
        d = lax.rem(me + k, n)
        return pltpu.make_async_remote_copy(
            src_ref=pay_ref.at[d],
            dst_ref=got.at[me],
            send_sem=pay_send.at[k],
            recv_sem=pay_recv.at[k],
            device_id=place(d),
            device_id_type=MESH,
        )

    def send_out(k, carry):
        outward(k).start()
        return carry

    lax.fori_loop(1, n, send_out, 0)

    for which, side, there, device in sides:
        recv = (xrecv, yrecv)[which]

        @pl.when(there)
        def _(which=which, side=side, device=device):
            pltpu.make_async_remote_copy(
                src_ref=(xsend, ysend)[which].at[side],
                dst_ref=(xrecv, yrecv)[which].at[side],
                send_sem=halo_send.at[2 * which + side],
                recv_sem=halo_recv.at[2 * which + side],
                device_id=device,
                device_id_type=MESH,
            ).wait()

        @pl.when(jnp.logical_not(there))
        def _(recv=recv, side=side):
            recv[side] = jnp.ones(recv.shape[1:], jnp.float32)

    west, east = gx == 0, gx == n_gx - 1
    south, north = gy == 0, gy == n_gy - 1
    flux_z[...] = jnp.zeros_like(flux_z)
    ext[...] = jnp.ones_like(ext)
    chunk = 32 if height % 32 == 0 else height
    tile = (chunk, width)
    lane = lax.broadcasted_iota(jnp.int32, tile, 1)
    row = lax.broadcasted_iota(jnp.int32, (chunk + 8, width), 0)
    first, last = lane == 0, lane == width - 1
    wall_low = jnp.logical_and(first, west)
    wall_high = jnp.logical_and(last, east)

    def plane(z, carry):
        above = jnp.minimum(z + 1, depth - 1)
        at_top = z == depth - 1
        here = conserve([prim(f, z, whole) for f in range(5)])
        for f in range(5):
            ext[f, 8 : 8 + height, :] = here[f]
        ext[5, 8 : 8 + height, :] = prim(2, z, whole)
        for side, at in ((0, 7), (1, 8 + height)):
            edge = [yrecv[side, f, pl.ds(z, 1), :] for f in range(5)]
            for f, q in enumerate(conserve(edge)):
                ext[f, at : at + 1, :] = q
            ext[5, at : at + 1, :] = edge[2]
        for y0 in range(0, height, chunk):
            rows = pl.ds(y0, chunk)
            own = [prim(f, z, rows) for f in range(5)]
            cons = conserve(own)
            change = [0.0] * 5
            up = [prim(f, above, rows) for f in range(5)]
            flux = face(cons, conserve(up), own[3], up[3], at_top)
            for f in range(5):
                change[f] = flux[f] - flux_z[f, rows, :]
                flux_z[f, rows, :] = flux[f]
            lower = [ext[f, pl.ds(7 + y0, chunk + 8), :] for f in range(6)]
            upper = [ext[f, pl.ds(8 + y0, chunk + 8), :] for f in range(6)]
            wall = False
            if y0 == 0:
                wall = jnp.logical_and(row == 0, south)
            if y0 + chunk == height:
                wall = jnp.logical_or(wall, jnp.logical_and(row == chunk, north))
            flux = face(lower[:5], upper[:5], lower[5], upper[5], wall)
            for f in range(5):
                change[f] = change[f] + (flux[f][1 : chunk + 1] - flux[f][:chunk])
            left, right = [], []
            for f in range(5):
                spot = f * depth + z
                left.append(
                    jnp.where(
                        first,
                        pltpu.roll(xrecv[0, rows, :], lax.rem(width - spot, width), 1),
                        pltpu.roll(own[f], 1, 1),
                    )
                )
                right.append(
                    jnp.where(
                        last,
                        pltpu.roll(xrecv[1, rows, :], width - 1 - spot, 1),
                        pltpu.roll(own[f], width - 1, 1),
                    )
                )
            flux = face(conserve(left), cons, left[1], own[1], wall_low)
            for f in range(5):
                change[f] = change[f] - flux[f]
            flux = face(cons, conserve(right), own[1], right[1], wall_high)
            for f in range(5):
                change[f] = change[f] + flux[f]
            fresh = [cons[f] - step_ratio * change[f] for f in range(5)]
            scale = 1.0 / fresh[0]
            out = pl.ds(z * height + y0, chunk)
            adv_ref[0, out, :] = fresh[0]
            for f in range(1, 5):
                adv_ref[f, out, :] = fresh[f] * scale
        return carry

    lax.fori_loop(0, depth, plane, 0)

    def pick(s, carry):
        for r in range(cap):
            b = jnp.maximum(map_ref[0, s * cap + r], 0)
            for f in range(5):
                picked[s, f * cap + r : f * cap + r + 1, :] = adv_ref[f, pl.ds(b, 1), :]
        return carry

    lax.fori_loop(0, n, pick, 0)

    def part(ref, s, j):
        return ref[s, j * cap : (j + 1) * cap, :]

    def couple(ref, s):
        g = part(picked, s, 0)
        scale = 1.0 / (g + part(ref, s, 0))
        for c in range(3):
            new_ref[s, c * cap : (c + 1) * cap, :] = (
                g * part(picked, s, 1 + c) + part(ref, s, 1 + c)
            ) * scale
        new_ref[s, 3 * cap : 4 * cap, :] = (g * part(picked, s, 4) + part(ref, s, 4)) / (
            g + part(ref, s, 5)
        )

    couple(pay_ref, me)
    home[me] = new_ref[me]

    def inward(k):
        d = lax.rem(me + n - k, n)
        return pltpu.make_async_remote_copy(
            src_ref=new_ref.at[d],
            dst_ref=home.at[me],
            send_sem=back_send.at[k],
            recv_sem=back_recv.at[k],
            device_id=place(d),
            device_id_type=MESH,
        )

    def answer(k, carry):
        d = lax.rem(me + n - k, n)
        outward(k).wait()
        couple(got, d)
        inward(k).start()
        return carry

    lax.fori_loop(1, n, answer, 0)

    def finish(k, carry):
        inward(k).wait()
        return carry

    lax.fori_loop(1, n, finish, 0)
    ret_ref[...] = home[...]


def final_kernel(
    cap, rank_ref, map_ref, ex_ref, adv_ref, new_ref, ret_ref, sums_ref, out_ref, solid_ref
):
    slots = rank_ref.shape[0]
    positions = map_ref.shape[1]
    out_ref[...] = adv_ref[...]
    factor = [coefficients(ex_ref, m) for m in range(2)]

    def scatter(i, carry):
        for u in range(cap):
            b = map_ref[0, i * cap + u]

            @pl.when(b >= 0)
            def _(u=u, b=b):
                for j in range(back):
                    out_ref[1 + j, pl.ds(b, 1), :] = new_ref[i, j * cap + u : j * cap + u + 1, :]

        return carry

    lax.fori_loop(0, positions // cap, scatter, 0)

    def solid(k, carry):
        v = rank_ref[k]
        live = v >= 0
        v = jnp.maximum(v, 0)
        s = v // cap
        r = v % cap
        rows = [ret_ref[s, pl.ds(j * cap + r, 1), :] for j in range(back)]
        total = sums_ref[k]
        for m in range(2):
            mass = total[8 * m : 8 * m + 1]
            for j in range(back):
                fac = ex_ref[m, j // 3]
                value = (total[8 * m + 1 + j : 8 * m + 2 + j] + fac * rows[j]) / (mass + fac)
                solid_ref[j, pl.ds(2 * k + m, 1), :] = jnp.where(live, value, 0.0)
        return carry

    lax.fori_loop(0, slots, solid, 0)


def per_device(
    n_gx,
    n_gy,
    gaseous_rho,
    gaseous_flow_vector,
    gaseous_kelvin,
    sender_tile_map,
    receiver_arrival_rank,
    bin_active_number,
    grain_inertia,
    grain_motion_vector,
    grain_kelvin,
    grain_voxel_number,
    grain_substance_label,
    exchange_factor,
):
    n = n_gx * n_gy
    depth, height, width = gaseous_rho.shape
    slots = grain_inertia.shape[0]
    cap = sender_tile_map.shape[1] // n
    blocks = depth * height
    f32 = jnp.float32
    shape = jax.ShapeDtypeStruct
    pay, sums = pl.pallas_call(
        functools.partial(bin_kernel, cap),
        out_shape=(shape((n, sent * cap, width), f32), shape((slots, 16, width), f32)),
        in_specs=[SMEM] * 3 + [VMEM] * 5,
        out_specs=(VMEM, VMEM),
        compiler_params=pltpu.CompilerParams(vmem_limit_bytes=limit),
        name="bin_grains",
    )(
        receiver_arrival_rank,
        bin_active_number,
        exchange_factor,
        grain_inertia,
        grain_motion_vector,
        grain_kelvin,
        grain_voxel_number,
        grain_substance_label,
    )
    dma = pltpu.SemaphoreType.DMA
    adv, new, ret = pl.pallas_call(
        functools.partial(grid_kernel, n_gx, n_gy),
        out_shape=(
            shape((5, blocks, width), f32),
            shape((n, back * cap, width), f32),
            shape((n, back * cap, width), f32),
        ),
        in_specs=[SMEM] + [VMEM] * 4,
        out_specs=(VMEM,) * 3,
        scratch_shapes=[
            pltpu.VMEM((2, height, width), f32),
            pltpu.VMEM((2, height, width), f32),
            pltpu.VMEM((2, 5, depth, width), f32),
            pltpu.VMEM((2, 5, depth, width), f32),
            pltpu.VMEM((n, sent * cap, width), f32),
            pltpu.VMEM((n, back * cap, width), f32),
            pltpu.VMEM((6, height + 16, width), f32),
            pltpu.VMEM((5, height, width), f32),
            pltpu.VMEM((n, 5 * cap, width), f32),
            dma((4,)),
            dma((4,)),
            dma((n,)),
            dma((n,)),
            dma((n,)),
            dma((n,)),
        ],
        compiler_params=pltpu.CompilerParams(
            collective_id=0, has_side_effects=True, vmem_limit_bytes=limit
        ),
        name="advance_and_couple",
    )(sender_tile_map, gaseous_rho, gaseous_flow_vector, gaseous_kelvin, pay)
    final, solid = pl.pallas_call(
        functools.partial(final_kernel, cap),
        out_shape=(shape((5, blocks, width), f32), shape((back, 2 * slots, width), f32)),
        in_specs=[SMEM] * 3 + [VMEM] * 4,
        out_specs=(VMEM, VMEM),
        compiler_params=pltpu.CompilerParams(vmem_limit_bytes=limit),
        name="place_results",
    )(receiver_arrival_rank, sender_tile_map, exchange_factor, adv, new, ret, sums)
    return (
        final.reshape(5, depth, height, width),
        solid.reshape(back, slots, 2, width),
    )


def solution(mesh):
    placed = (
        P(None, "gy", "gx"),
        P(None, None, "gy", "gx"),
        P(None, "gy", "gx"),
        P(("gx", "gy"), None),
        P(("gx", "gy")),
        P(("gx", "gy")),
        P(("gx", "gy"), None),
        P(None, ("gx", "gy"), None),
        P(("gx", "gy"), None),
        P(("gx", "gy"), None),
        P(("gx", "gy"), None),
        P(),
    )
    return jax.shard_map(
        functools.partial(per_device, mesh.shape["gx"], mesh.shape["gy"]),
        mesh=mesh,
        in_specs=placed,
        out_specs=(P(None, None, "gy", "gx"), P(None, ("gx", "gy"), None, None)),
        check_vma=False,
    )
```

```python
import functools

import jax
import jax.numpy as jnp
from jax import lax
from jax.experimental import pallas as pl
from jax.experimental.pallas import tpu as pltpu
from jax.sharding import PartitionSpec as P

MESH = pl.DeviceIdType.MESH
VMEM = pl.BlockSpec(memory_space=pltpu.VMEM)
ANY = pl.BlockSpec(memory_space=pl.ANY)
SMEM = pl.BlockSpec(memory_space=pltpu.SMEM)
step_ratio = 0.08
limit = 24 * 1024 * 1024
sent = 6
back = 4


def coefficients(ex_ref, m):
    rows = lax.broadcasted_iota(jnp.int32, (8, 128), 0)
    return jnp.where(rows < 4, ex_ref[m, 0], ex_ref[m, 1])


def bin_kernel(
    cap, rank_ref, count_ref, ex_ref, mass_ref, vel_ref, temp_ref, vox_ref, lab_ref, pay_ref, calm_ref, pull_ref
):
    slots, padding = mass_ref.shape
    width = pay_ref.shape[2]
    pay_ref[...] = jnp.zeros_like(pay_ref)
    rows = lax.broadcasted_iota(jnp.int32, (8, padding), 0)
    lane = lax.broadcasted_iota(jnp.int32, (1, padding), 1)
    cells = lax.broadcasted_iota(jnp.int32, (width, padding), 0)
    factor = [coefficients(ex_ref, m) for m in range(2)]
    unroll = 8
    spare = (pay_ref.shape[0] - 1) * cap

    def body(i, carry):
        for u in range(unroll):
            k = i * unroll + u
            here = pl.ds(k, 1)
            mass = jnp.where(lane < count_ref[k], mass_ref[here, :], 0.0)
            base = jnp.where(rows == 4, temp_ref[here, :], 1.0)
            for c in range(3):
                base = jnp.where(rows == c + 1, vel_ref[c, here, :], base)
            base = base * mass
            label = lab_ref[here, :]
            values = jnp.concatenate(
                [jnp.where(label == 0, base, 0.0), jnp.where(label == 1, base, 0.0)], 0
            )
            high = values.astype(jnp.bfloat16)
            low = (values - high.astype(jnp.float32)).astype(jnp.bfloat16)
            onehot = jnp.where(cells == vox_ref[here, :], 1.0, 0.0).astype(jnp.bfloat16)
            total = lax.dot_general(
                jnp.concatenate([high, low], 0),
                onehot,
                (((1,), (1,)), ((), ())),
                preferred_element_type=jnp.float32,
            )
            total = total[:16] + total[16:]
            pay = 0.0
            v = rank_ref[k]
            live = jnp.where(v >= 0, 1.0, 0.0)
            for m in range(2):
                part = total[8 * m : 8 * m + 8]
                scale = 1.0 / (part[0:1] + factor[m])
                pull = factor[m] * scale
                pay = pay + pull * part
                calm = part * scale * live
                pull = pull * live
                for j in range(back):
                    calm_ref[j, pl.ds(2 * k + m, 1), :] = calm[1 + j : 2 + j]
                for j in range(2):
                    pull_ref[j, pl.ds(2 * k + m, 1), :] = pull[1 + 3 * j : 2 + 3 * j]
            v = jnp.where(v >= 0, v, spare)
            s = v // cap
            r = v % cap
            for j in range(sent):
                pay_ref[s, pl.ds(j * cap + r, 1), :] = pay[j : j + 1]

        return carry

    lax.fori_loop(0, slots // unroll, body, 0)


def face(a, b, ua, ub, wall):
    speed = 0.5 * (ua + ub) - (2.0 * step_ratio) * (b[4] - a[4]) / (a[0] + b[0])
    speed = jnp.where(wall, 0.0, speed)
    ahead = speed > 0
    return [speed * jnp.where(ahead, x, y) for x, y in zip(a, b)]


def conserve(prim):
    rho = prim[0]
    return [rho] + [rho * q for q in prim[1:]]


def grid_kernel(
    n_gx,
    n_gy,
    map_ref,
    rho_ref,
    vel_ref,
    temp_ref,
    pay_ref,
    adv_ref,
    new_ref,
    ret_ref,
    xsend,
    xrecv,
    ysend,
    yrecv,
    got,
    home,
    ext,
    flux_z,
    picked,
    halo_send,
    halo_recv,
    pay_send,
    pay_recv,
    back_send,
    back_recv,
):
    n = n_gx * n_gy
    depth, height, width = rho_ref.shape
    cap = map_ref.shape[1] // n
    gx = lax.axis_index("gx")
    gy = lax.axis_index("gy")
    me = gx * n_gy + gy

    def place(d):
        return (d // n_gy, lax.rem(d, n_gy))

    barrier = pltpu.get_barrier_semaphore()

    def greet(k, carry):
        d = lax.rem(me + k, n)
        pl.semaphore_signal(barrier, inc=1, device_id=place(d), device_id_type=MESH)
        return carry

    lax.fori_loop(1, n, greet, 0)

    def prim(f, z, rows):
        if f == 0:
            return rho_ref[z, rows, :]
        if f == 4:
            return temp_ref[z, rows, :]
        return vel_ref[f - 1, z, rows, :]

    whole = pl.ds(0, height)
    lanes = lax.broadcasted_iota(jnp.int32, (height, width), 1)

    def pack(z, carry):
        low, high = carry
        for f in range(5):
            spot = f * depth + z
            x = prim(f, z, whole)
            ysend[0, f, pl.ds(z, 1), :] = x[0:1]
            ysend[1, f, pl.ds(z, 1), :] = x[height - 1 : height]
            low = jnp.where(lanes == spot, pltpu.roll(x, spot, 1), low)
            high = jnp.where(lanes == spot, pltpu.roll(x, spot + 1, 1), high)
        return (low, high)

    zero = jnp.zeros((height, width), jnp.float32)
    low, high = lax.fori_loop(0, depth, pack, (zero, zero))
    xsend[0] = low
    xsend[1] = high
    pl.semaphore_wait(barrier, n - 1)

    def halo(which, side, device):
        src, dst = ((xsend, xrecv), (ysend, yrecv))[which]
        return pltpu.make_async_remote_copy(
            src_ref=src.at[side],
            dst_ref=dst.at[1 - side],
            send_sem=halo_send.at[2 * which + side],
            recv_sem=halo_recv.at[2 * which + 1 - side],
            device_id=device,
            device_id_type=MESH,
        )

    sides = (
        (0, 0, gx > 0, (gx - 1, gy)),
        (0, 1, gx < n_gx - 1, (gx + 1, gy)),
        (1, 0, gy > 0, (gx, gy - 1)),
        (1, 1, gy < n_gy - 1, (gx, gy + 1)),
    )
    for which, side, there, device in sides:

        @pl.when(there)
        def _(which=which, side=side, device=device):
            halo(which, side, device).start()

    def outward(k):
        d = lax.rem(me + k, n)
        return pltpu.make_async_remote_copy(
            src_ref=pay_ref.at[d],
            dst_ref=got.at[me],
            send_sem=pay_send.at[k],
            recv_sem=pay_recv.at[k],
            device_id=place(d),
            device_id_type=MESH,
        )

    def send_out(k, carry):
        outward(k).start()
        return carry

    lax.fori_loop(1, n, send_out, 0)

    for which, side, there, device in sides:
        recv = (xrecv, yrecv)[which]

        @pl.when(there)
        def _(which=which, side=side, device=device):
            pltpu.make_async_remote_copy(
                src_ref=(xsend, ysend)[which].at[side],
                dst_ref=(xrecv, yrecv)[which].at[side],
                send_sem=halo_send.at[2 * which + side],
                recv_sem=halo_recv.at[2 * which + side],
                device_id=device,
                device_id_type=MESH,
            ).wait()

        @pl.when(jnp.logical_not(there))
        def _(recv=recv, side=side):
            recv[side] = jnp.ones(recv.shape[1:], jnp.float32)

    west, east = gx == 0, gx == n_gx - 1
    south, north = gy == 0, gy == n_gy - 1
    flux_z[...] = jnp.zeros_like(flux_z)
    ext[...] = jnp.ones_like(ext)
    chunk = 32 if height % 32 == 0 else height
    tile = (chunk, width)
    lane = lax.broadcasted_iota(jnp.int32, tile, 1)
    row = lax.broadcasted_iota(jnp.int32, (chunk + 8, width), 0)
    first, last = lane == 0, lane == width - 1
    wall_low = jnp.logical_and(first, west)
    wall_high = jnp.logical_and(last, east)

    def plane(z, carry):
        above = jnp.minimum(z + 1, depth - 1)
        at_top = z == depth - 1
        here = conserve([prim(f, z, whole) for f in range(5)])
        for f in range(5):
            ext[f, 8 : 8 + height, :] = here[f]
        ext[5, 8 : 8 + height, :] = prim(2, z, whole)
        for side, at in ((0, 7), (1, 8 + height)):
            edge = [yrecv[side, f, pl.ds(z, 1), :] for f in range(5)]
            for f, q in enumerate(conserve(edge)):
                ext[f, at : at + 1, :] = q
            ext[5, at : at + 1, :] = edge[2]
        for y0 in range(0, height, chunk):
            rows = pl.ds(y0, chunk)
            own = [prim(f, z, rows) for f in range(5)]
            cons = conserve(own)
            change = [0.0] * 5
            up = [prim(f, above, rows) for f in range(5)]
            flux = face(cons, conserve(up), own[3], up[3], at_top)
            for f in range(5):
                change[f] = flux[f] - flux_z[f, rows, :]
                flux_z[f, rows, :] = flux[f]
            lower = [ext[f, pl.ds(7 + y0, chunk + 8), :] for f in range(6)]
            upper = [ext[f, pl.ds(8 + y0, chunk + 8), :] for f in range(6)]
            wall = False
            if y0 == 0:
                wall = jnp.logical_and(row == 0, south)
            if y0 + chunk == height:
                wall = jnp.logical_or(wall, jnp.logical_and(row == chunk, north))
            flux = face(lower[:5], upper[:5], lower[5], upper[5], wall)
            for f in range(5):
                change[f] = change[f] + (flux[f][1 : chunk + 1] - flux[f][:chunk])
            left, right = [], []
            for f in range(5):
                spot = f * depth + z
                left.append(
                    jnp.where(
                        first,
                        pltpu.roll(xrecv[0, rows, :], lax.rem(width - spot, width), 1),
                        pltpu.roll(own[f], 1, 1),
                    )
                )
                right.append(
                    jnp.where(
                        last,
                        pltpu.roll(xrecv[1, rows, :], width - 1 - spot, 1),
                        pltpu.roll(own[f], width - 1, 1),
                    )
                )
            flux = face(conserve(left), cons, left[1], own[1], wall_low)
            for f in range(5):
                change[f] = change[f] - flux[f]
            flux = face(cons, conserve(right), own[1], right[1], wall_high)
            for f in range(5):
                change[f] = change[f] + flux[f]
            fresh = [cons[f] - step_ratio * change[f] for f in range(5)]
            scale = 1.0 / fresh[0]
            out = pl.ds(z * height + y0, chunk)
            adv_ref[0, out, :] = fresh[0]
            for f in range(1, 5):
                adv_ref[f, out, :] = fresh[f] * scale
        return carry

    lax.fori_loop(0, depth, plane, 0)

    def pick(s, carry):
        for r in range(cap):
            b = jnp.maximum(map_ref[0, s * cap + r], 0)
            for f in range(5):
                picked[s, f * cap + r : f * cap + r + 1, :] = adv_ref[f, pl.ds(b, 1), :]
        return carry

    lax.fori_loop(0, n, pick, 0)

    def part(ref, s, j):
        return ref[s, j * cap : (j + 1) * cap, :]

    def couple(ref, s):
        g = part(picked, s, 0)
        scale = 1.0 / (g + part(ref, s, 0))
        for c in range(3):
            new_ref[s, c * cap : (c + 1) * cap, :] = (
                g * part(picked, s, 1 + c) + part(ref, s, 1 + c)
            ) * scale
        new_ref[s, 3 * cap : 4 * cap, :] = (g * part(picked, s, 4) + part(ref, s, 4)) / (
            g + part(ref, s, 5)
        )

    couple(pay_ref, me)
    home[me] = new_ref[me]

    def inward(k):
        d = lax.rem(me + n - k, n)
        return pltpu.make_async_remote_copy(
            src_ref=new_ref.at[d],
            dst_ref=home.at[me],
            send_sem=back_send.at[k],
            recv_sem=back_recv.at[k],
            device_id=place(d),
            device_id_type=MESH,
        )

    def answer(k, carry):
        d = lax.rem(me + n - k, n)
        outward(k).wait()
        couple(got, d)
        inward(k).start()
        return carry

    lax.fori_loop(1, n, answer, 0)

    def finish(k, carry):
        inward(k).wait()
        return carry

    lax.fori_loop(1, n, finish, 0)
    ret_ref[...] = home[...]


def final_kernel(
    cap, rank_ref, map_ref, adv_ref, new_ref, ret_ref, calm_ref, pull_ref, out_ref, solid_ref, held, sem
):
    slots = rank_ref.shape[0]
    positions = map_ref.shape[1]
    fields, blocks, width = adv_ref.shape

    def whole(f, inward):
        here = held.at[f, pl.ds(0, blocks), :]
        if inward:
            return pltpu.make_async_copy(adv_ref.at[f], here, sem.at[f])
        return pltpu.make_async_copy(here, out_ref.at[f], sem.at[f])

    for f in range(fields):
        whole(f, True).start()
    unroll = 8

    def solid(i, carry):
        for u in range(unroll):
            k = i * unroll + u
            v = jnp.maximum(rank_ref[k], 0)
            s = v // cap
            r = v % cap
            for j in range(back):
                row = ret_ref[s, pl.ds(j * cap + r, 1), :]
                solid_ref[j, pl.ds(2 * k, 2), :] = jnp.broadcast_to(row, (2, width))
        return carry

    lax.fori_loop(0, slots // unroll, solid, 0)
    for j in range(back):
        solid_ref[j] = calm_ref[j] + pull_ref[j // 3] * solid_ref[j]
    for f in range(fields):
        whole(f, True).wait()
    whole(0, False).start()

    def scatter(i, carry):
        for u in range(cap):
            b = map_ref[0, i * cap + u]
            b = jnp.where(b >= 0, b, blocks)
            for j in range(back):
                held[1 + j, pl.ds(b, 1), :] = new_ref[i, j * cap + u : j * cap + u + 1, :]
        return carry

    lax.fori_loop(0, positions // cap, scatter, 0)
    for f in range(1, fields):
        whole(f, False).start()
    for f in range(fields):
        whole(f, False).wait()


def per_device(
    n_gx,
    n_gy,
    gaseous_rho,
    gaseous_flow_vector,
    gaseous_kelvin,
    sender_tile_map,
    receiver_arrival_rank,
    bin_active_number,
    grain_inertia,
    grain_motion_vector,
    grain_kelvin,
    grain_voxel_number,
    grain_substance_label,
    exchange_factor,
):
    n = n_gx * n_gy
    depth, height, width = gaseous_rho.shape
    slots = grain_inertia.shape[0]
    cap = sender_tile_map.shape[1] // n
    blocks = depth * height
    f32 = jnp.float32
    shape = jax.ShapeDtypeStruct
    pay, calm, pull = pl.pallas_call(
        functools.partial(bin_kernel, cap),
        out_shape=(
            shape((n + 1, sent * cap, width), f32),
            shape((back, 2 * slots, width), f32),
            shape((2, 2 * slots, width), f32),
        ),
        in_specs=[SMEM] * 3 + [VMEM] * 5,
        out_specs=(VMEM,) * 3,
        compiler_params=pltpu.CompilerParams(vmem_limit_bytes=limit),
        name="bin_grains",
    )(
        receiver_arrival_rank,
        bin_active_number,
        exchange_factor,
        grain_inertia,
        grain_motion_vector,
        grain_kelvin,
        grain_voxel_number,
        grain_substance_label,
    )
    dma = pltpu.SemaphoreType.DMA
    adv, new, ret = pl.pallas_call(
        functools.partial(grid_kernel, n_gx, n_gy),
        out_shape=(
            shape((5, blocks, width), f32),
            shape((n, back * cap, width), f32),
            shape((n, back * cap, width), f32),
        ),
        in_specs=[SMEM] + [VMEM] * 4,
        out_specs=(VMEM,) * 3,
        scratch_shapes=[
            pltpu.VMEM((2, height, width), f32),
            pltpu.VMEM((2, height, width), f32),
            pltpu.VMEM((2, 5, depth, width), f32),
            pltpu.VMEM((2, 5, depth, width), f32),
            pltpu.VMEM((n, sent * cap, width), f32),
            pltpu.VMEM((n, back * cap, width), f32),
            pltpu.VMEM((6, height + 16, width), f32),
            pltpu.VMEM((5, height, width), f32),
            pltpu.VMEM((n, 5 * cap, width), f32),
            dma((4,)),
            dma((4,)),
            dma((n,)),
            dma((n,)),
            dma((n,)),
            dma((n,)),
        ],
        compiler_params=pltpu.CompilerParams(
            collective_id=0, has_side_effects=True, vmem_limit_bytes=limit
        ),
        name="advance_and_couple",
    )(sender_tile_map, gaseous_rho, gaseous_flow_vector, gaseous_kelvin, pay)
    final, solid = pl.pallas_call(
        functools.partial(final_kernel, cap),
        out_shape=(shape((5, blocks, width), f32), shape((back, 2 * slots, width), f32)),
        in_specs=[SMEM] * 2 + [ANY] + [VMEM] * 4,
        out_specs=(ANY, VMEM),
        scratch_shapes=[pltpu.VMEM((5, blocks + 8, width), f32), dma((5,))],
        compiler_params=pltpu.CompilerParams(vmem_limit_bytes=limit),
        name="place_results",
    )(receiver_arrival_rank, sender_tile_map, adv, new, ret, calm, pull)
    return (
        final.reshape(5, depth, height, width),
        solid.reshape(back, slots, 2, width),
    )


def solution(mesh):
    placed = (
        P(None, "gy", "gx"),
        P(None, None, "gy", "gx"),
        P(None, "gy", "gx"),
        P(("gx", "gy"), None),
        P(("gx", "gy")),
        P(("gx", "gy")),
        P(("gx", "gy"), None),
        P(None, ("gx", "gy"), None),
        P(("gx", "gy"), None),
        P(("gx", "gy"), None),
        P(("gx", "gy"), None),
        P(),
    )
    return jax.shard_map(
        functools.partial(per_device, mesh.shape["gx"], mesh.shape["gy"]),
        mesh=mesh,
        in_specs=placed,
        out_specs=(P(None, None, "gy", "gx"), P(None, ("gx", "gy"), None, None)),
        check_vma=False,
    )
```

```python
import functools

import jax
import jax.numpy as jnp
from jax import lax
from jax.experimental import pallas as pl
from jax.experimental.pallas import tpu as pltpu
from jax.sharding import PartitionSpec as P

MESH = pl.DeviceIdType.MESH
VMEM = pl.BlockSpec(memory_space=pltpu.VMEM)
HBM = pl.BlockSpec(memory_space=pltpu.HBM)
ANY = pl.BlockSpec(memory_space=pl.ANY)
SMEM = pl.BlockSpec(memory_space=pltpu.SMEM)
step_ratio = 0.08
limit = 24 * 1024 * 1024
sent = 6
back = 4


def coefficients(ex_ref, m):
    rows = lax.broadcasted_iota(jnp.int32, (8, 128), 0)
    return jnp.where(rows < 4, ex_ref[m, 0], ex_ref[m, 1])


def bin_grains(
    rank_ref, count_ref, ex_ref, mass_ref, vel_ref, temp_ref, vox_ref, lab_ref, dense, calm_ref, pull_ref
):
    slots, padding = mass_ref.shape
    width = dense.shape[2]
    rows = lax.broadcasted_iota(jnp.int32, (8, padding), 0)
    lane = lax.broadcasted_iota(jnp.int32, (1, padding), 1)
    cells = lax.broadcasted_iota(jnp.int32, (width, padding), 0)
    factor = [coefficients(ex_ref, m) for m in range(2)]
    unroll = 8

    def body(i, carry):
        for u in range(unroll):
            k = i * unroll + u
            here = pl.ds(k, 1)
            mass = jnp.where(lane < count_ref[0, k], mass_ref[here, :], 0.0)
            base = jnp.where(rows == 4, temp_ref[here, :], 1.0)
            for c in range(3):
                base = jnp.where(rows == c + 1, vel_ref[c, here, :], base)
            base = base * mass
            label = lab_ref[here, :]
            values = jnp.concatenate(
                [jnp.where(label == 0, base, 0.0), jnp.where(label == 1, base, 0.0)], 0
            )
            onehot = jnp.where(cells == vox_ref[here, :], 1.0, 0.0).astype(jnp.bfloat16)
            total = lax.dot_general(
                jnp.concatenate(split(values, 2), 0),
                onehot,
                (((1,), (1,)), ((), ())),
                preferred_element_type=jnp.float32,
            )
            total = total[:16] + total[16:]
            pay = 0.0
            live = jnp.where(rank_ref[0, k] >= 0, 1.0, 0.0)
            for m in range(2):
                part = total[8 * m : 8 * m + 8]
                scale = 1.0 / (part[0:1] + factor[m])
                pull = factor[m] * scale
                pay = pay + pull * part
                calm = part * scale * live
                pull = pull * live
                for j in range(back):
                    calm_ref[j, pl.ds(2 * k + m, 1), :] = calm[1 + j : 2 + j]
                for j in range(2):
                    pull_ref[j, pl.ds(2 * k + m, 1), :] = pull[1 + 3 * j : 2 + 3 * j]
            for j in range(sent):
                dense[j, here, :] = pay[j : j + 1]
        return carry

    lax.fori_loop(0, slots // unroll, body, 0)


def split(x, parts):
    out = []
    for _ in range(parts):
        out.append(x.astype(jnp.bfloat16))
        x = x - out[-1].astype(jnp.float32)
    return out


def place_pay(rank_row, dense, pay_ref, cap):
    n = pay_ref.shape[0]
    slots = dense.shape[1]
    position = lax.broadcasted_iota(jnp.int32, (n * cap, slots), 0)
    onehot = jnp.where(position == rank_row[...], 1.0, 0.0).astype(jnp.bfloat16)
    for j in range(sent):
        total = 0.0
        for piece in split(dense[j], 3):
            total = total + jnp.dot(onehot, piece, preferred_element_type=jnp.float32)
        for s in range(n):
            pay_ref[s, j * cap : (j + 1) * cap, :] = total[s * cap : (s + 1) * cap]


def face(a, b, ua, ub, wall):
    speed = 0.5 * (ua + ub) - (2.0 * step_ratio) * (b[4] - a[4]) / (a[0] + b[0])
    speed = jnp.where(wall, 0.0, speed)
    ahead = speed > 0
    return [speed * jnp.where(ahead, x, y) for x, y in zip(a, b)]


def conserve(prim):
    rho = prim[0]
    return [rho] + [rho * q for q in prim[1:]]


def grid_kernel(
    n_gx,
    n_gy,
    rho_hbm,
    vel_hbm,
    temp_hbm,
    map_hbm,
    rank_hbm,
    count_hbm,
    mass_hbm,
    motion_hbm,
    kelvin_hbm,
    vox_hbm,
    lab_hbm,
    ex_hbm,
    adv_ref,
    new_ref,
    ret_ref,
    calm_ref,
    pull_ref,
    rho_ref,
    vel_ref,
    temp_ref,
    mass_ref,
    motion_ref,
    kelvin_ref,
    vox_ref,
    lab_ref,
    rank_row,
    map_ref,
    rank_ref,
    count_ref,
    ex_ref,
    dense,
    pay_ref,
    xsend,
    xrecv,
    ysend,
    yrecv,
    got,
    home,
    ext,
    flux_z,
    picked,
    load_sem,
    halo_send,
    halo_recv,
    pay_send,
    pay_recv,
    back_send,
    back_recv,
):
    n = n_gx * n_gy
    depth, height, width = rho_ref.shape
    cap = map_hbm.shape[1] // n
    gx = lax.axis_index("gx")
    gy = lax.axis_index("gy")
    me = gx * n_gy + gy

    def place(d):
        return (d // n_gy, lax.rem(d, n_gy))

    def ahead(k):
        x = lax.rem(gx + lax.rem(k, n_gx), n_gx)
        return x * n_gy + lax.rem(gy + k // n_gx, n_gy)

    def behind(k):
        x = lax.rem(gx + n_gx - lax.rem(k, n_gx), n_gx)
        return x * n_gy + lax.rem(gy + n_gy - k // n_gx, n_gy)

    barrier = pltpu.get_barrier_semaphore()

    def greet(k, carry):
        d = lax.rem(me + k, n)
        pl.semaphore_signal(barrier, inc=1, device_id=place(d), device_id_type=MESH)
        return carry

    loads = [
        pltpu.make_async_copy(src, dst, load_sem.at[i])
        for i, (src, dst) in enumerate(
            (
                (rho_hbm, rho_ref),
                (vel_hbm, vel_ref),
                (temp_hbm, temp_ref),
                (mass_hbm, mass_ref),
                (motion_hbm, motion_ref),
                (kelvin_hbm, kelvin_ref),
                (vox_hbm, vox_ref),
                (lab_hbm, lab_ref),
                (rank_hbm, rank_row),
                (map_hbm, map_ref),
                (rank_hbm, rank_ref),
                (count_hbm, count_ref),
                (ex_hbm, ex_ref),
            )
        )
    ]
    for load in loads:
        load.start()
    lax.fori_loop(1, n, greet, 0)
    for load in loads[:3]:
        load.wait()

    def prim(f, z, rows):
        if f == 0:
            return rho_ref[z, rows, :]
        if f == 4:
            return temp_ref[z, rows, :]
        return vel_ref[f - 1, z, rows, :]

    whole = pl.ds(0, height)
    lanes = lax.broadcasted_iota(jnp.int32, (height, width), 1)

    def pack(z, carry):
        low, high = carry
        for f in range(5):
            spot = f * depth + z
            x = prim(f, z, whole)
            ysend[0, f, pl.ds(z, 1), :] = x[0:1]
            ysend[1, f, pl.ds(z, 1), :] = x[height - 1 : height]
            low = jnp.where(lanes == spot, pltpu.roll(x, spot, 1), low)
            high = jnp.where(lanes == spot, pltpu.roll(x, spot + 1, 1), high)
        return (low, high)

    zero = jnp.zeros((height, width), jnp.float32)
    low, high = lax.fori_loop(0, depth, pack, (zero, zero))
    xsend[0] = low
    xsend[1] = high
    pl.semaphore_wait(barrier, n - 1)

    def halo(which, side, device):
        src, dst = ((xsend, xrecv), (ysend, yrecv))[which]
        return pltpu.make_async_remote_copy(
            src_ref=src.at[side],
            dst_ref=dst.at[1 - side],
            send_sem=halo_send.at[2 * which + side],
            recv_sem=halo_recv.at[2 * which + 1 - side],
            device_id=device,
            device_id_type=MESH,
        )

    sides = (
        (0, 0, gx > 0, (gx - 1, gy)),
        (0, 1, gx < n_gx - 1, (gx + 1, gy)),
        (1, 0, gy > 0, (gx, gy - 1)),
        (1, 1, gy < n_gy - 1, (gx, gy + 1)),
    )
    for which, side, there, device in sides:

        @pl.when(there)
        def _(which=which, side=side, device=device):
            halo(which, side, device).start()

    for load in loads[3:]:
        load.wait()
    bin_grains(
        rank_ref,
        count_ref,
        ex_ref,
        mass_ref,
        motion_ref,
        kelvin_ref,
        vox_ref,
        lab_ref,
        dense,
        calm_ref,
        pull_ref,
    )
    place_pay(rank_row, dense, pay_ref, cap)

    def outward(k):
        d = ahead(k)
        return pltpu.make_async_remote_copy(
            src_ref=pay_ref.at[d],
            dst_ref=got.at[me],
            send_sem=pay_send.at[k],
            recv_sem=pay_recv.at[k],
            device_id=place(d),
            device_id_type=MESH,
        )

    def send_out(k, carry):
        outward(k).start()
        return carry

    lax.fori_loop(1, n, send_out, 0)

    for which, side, there, device in sides:
        recv = (xrecv, yrecv)[which]

        @pl.when(there)
        def _(which=which, side=side, device=device):
            pltpu.make_async_remote_copy(
                src_ref=(xsend, ysend)[which].at[side],
                dst_ref=(xrecv, yrecv)[which].at[side],
                send_sem=halo_send.at[2 * which + side],
                recv_sem=halo_recv.at[2 * which + side],
                device_id=device,
                device_id_type=MESH,
            ).wait()

        @pl.when(jnp.logical_not(there))
        def _(recv=recv, side=side):
            recv[side] = jnp.ones(recv.shape[1:], jnp.float32)

    west, east = gx == 0, gx == n_gx - 1
    south, north = gy == 0, gy == n_gy - 1
    flux_z[...] = jnp.zeros_like(flux_z)
    ext[...] = jnp.ones_like(ext)
    chunk = 32 if height % 32 == 0 else height
    tile = (chunk, width)
    lane = lax.broadcasted_iota(jnp.int32, tile, 1)
    row = lax.broadcasted_iota(jnp.int32, (chunk + 8, width), 0)
    first, last = lane == 0, lane == width - 1
    wall_low = jnp.logical_and(first, west)
    wall_high = jnp.logical_and(last, east)

    def plane(z, carry):
        above = jnp.minimum(z + 1, depth - 1)
        at_top = z == depth - 1
        here = conserve([prim(f, z, whole) for f in range(5)])
        for f in range(5):
            ext[f, 8 : 8 + height, :] = here[f]
        ext[5, 8 : 8 + height, :] = prim(2, z, whole)
        for side, at in ((0, 7), (1, 8 + height)):
            edge = [yrecv[side, f, pl.ds(z, 1), :] for f in range(5)]
            for f, q in enumerate(conserve(edge)):
                ext[f, at : at + 1, :] = q
            ext[5, at : at + 1, :] = edge[2]
        for y0 in range(0, height, chunk):
            rows = pl.ds(y0, chunk)
            own = [prim(f, z, rows) for f in range(5)]
            cons = conserve(own)
            change = [0.0] * 5
            up = [prim(f, above, rows) for f in range(5)]
            flux = face(cons, conserve(up), own[3], up[3], at_top)
            for f in range(5):
                change[f] = flux[f] - flux_z[f, rows, :]
                flux_z[f, rows, :] = flux[f]
            lower = [ext[f, pl.ds(7 + y0, chunk + 8), :] for f in range(6)]
            upper = [ext[f, pl.ds(8 + y0, chunk + 8), :] for f in range(6)]
            wall = False
            if y0 == 0:
                wall = jnp.logical_and(row == 0, south)
            if y0 + chunk == height:
                wall = jnp.logical_or(wall, jnp.logical_and(row == chunk, north))
            flux = face(lower[:5], upper[:5], lower[5], upper[5], wall)
            for f in range(5):
                change[f] = change[f] + (flux[f][1 : chunk + 1] - flux[f][:chunk])
            left, right = [], []
            for f in range(5):
                spot = f * depth + z
                left.append(
                    jnp.where(
                        first,
                        pltpu.roll(xrecv[0, rows, :], lax.rem(width - spot, width), 1),
                        pltpu.roll(own[f], 1, 1),
                    )
                )
                right.append(
                    jnp.where(
                        last,
                        pltpu.roll(xrecv[1, rows, :], width - 1 - spot, 1),
                        pltpu.roll(own[f], width - 1, 1),
                    )
                )
            flux = face(conserve(left), cons, left[1], own[1], wall_low)
            for f in range(5):
                change[f] = change[f] - flux[f]
            flux = face(cons, conserve(right), own[1], right[1], wall_high)
            for f in range(5):
                change[f] = change[f] + flux[f]
            fresh = [cons[f] - step_ratio * change[f] for f in range(5)]
            scale = 1.0 / fresh[0]
            out = pl.ds(z * height + y0, chunk)
            adv_ref[0, out, :] = fresh[0]
            for f in range(1, 5):
                adv_ref[f, out, :] = fresh[f] * scale
        return carry

    lax.fori_loop(0, depth, plane, 0)

    def pick(s, carry):
        for r in range(cap):
            b = jnp.maximum(map_ref[0, s * cap + r], 0)
            for f in range(5):
                picked[s, f * cap + r : f * cap + r + 1, :] = adv_ref[f, pl.ds(b, 1), :]
        return carry

    lax.fori_loop(0, n, pick, 0)

    def part(ref, s, j):
        return ref[s, j * cap : (j + 1) * cap, :]

    def couple(ref, s):
        g = part(picked, s, 0)
        scale = 1.0 / (g + part(ref, s, 0))
        for c in range(3):
            new_ref[s, c * cap : (c + 1) * cap, :] = (
                g * part(picked, s, 1 + c) + part(ref, s, 1 + c)
            ) * scale
        new_ref[s, 3 * cap : 4 * cap, :] = (g * part(picked, s, 4) + part(ref, s, 4)) / (
            g + part(ref, s, 5)
        )

    couple(pay_ref, me)
    home[me] = new_ref[me]

    def inward(k):
        d = behind(k)
        return pltpu.make_async_remote_copy(
            src_ref=new_ref.at[d],
            dst_ref=home.at[me],
            send_sem=back_send.at[k],
            recv_sem=back_recv.at[k],
            device_id=place(d),
            device_id_type=MESH,
        )

    def answer(k, carry):
        d = behind(k)
        outward(k).wait()
        couple(got, d)
        inward(k).start()
        return carry

    lax.fori_loop(1, n, answer, 0)

    def finish(k, carry):
        inward(k).wait()
        return carry

    lax.fori_loop(1, n, finish, 0)
    ret_ref[...] = home[...]


def final_kernel(
    cap, rank_ref, map_ref, adv_ref, new_ref, ret_ref, calm_ref, pull_ref, out_ref, solid_ref, held, sem
):
    slots = rank_ref.shape[0]
    positions = map_ref.shape[1]
    fields, blocks, width = adv_ref.shape

    def whole(f, inward):
        here = held.at[f, pl.ds(0, blocks), :]
        if inward:
            return pltpu.make_async_copy(adv_ref.at[f], here, sem.at[f])
        return pltpu.make_async_copy(here, out_ref.at[f], sem.at[f])

    for f in range(fields):
        whole(f, True).start()
    unroll = 8

    def solid(i, carry):
        for u in range(unroll):
            k = i * unroll + u
            v = jnp.maximum(rank_ref[k], 0)
            s = v // cap
            r = v % cap
            for j in range(back):
                row = ret_ref[s, pl.ds(j * cap + r, 1), :]
                solid_ref[j, pl.ds(2 * k, 2), :] = jnp.broadcast_to(row, (2, width))
        return carry

    lax.fori_loop(0, slots // unroll, solid, 0)
    for j in range(back):
        solid_ref[j] = calm_ref[j] + pull_ref[j // 3] * solid_ref[j]
    for f in range(fields):
        whole(f, True).wait()
    whole(0, False).start()

    def scatter(i, carry):
        for u in range(cap):
            b = map_ref[0, i * cap + u]
            b = jnp.where(b >= 0, b, blocks)
            for j in range(back):
                held[1 + j, pl.ds(b, 1), :] = new_ref[i, j * cap + u : j * cap + u + 1, :]
        return carry

    lax.fori_loop(0, positions // cap, scatter, 0)
    for f in range(1, fields):
        whole(f, False).start()
    for f in range(fields):
        whole(f, False).wait()


def per_device(
    n_gx,
    n_gy,
    gaseous_rho,
    gaseous_flow_vector,
    gaseous_kelvin,
    sender_tile_map,
    receiver_arrival_rank,
    bin_active_number,
    grain_inertia,
    grain_motion_vector,
    grain_kelvin,
    grain_voxel_number,
    grain_substance_label,
    exchange_factor,
):
    n = n_gx * n_gy
    depth, height, width = gaseous_rho.shape
    slots, padding = grain_inertia.shape
    cap = sender_tile_map.shape[1] // n
    blocks = depth * height
    f32, i32 = jnp.float32, jnp.int32
    shape = jax.ShapeDtypeStruct
    dma = pltpu.SemaphoreType.DMA
    adv, new, ret, calm, pull = pl.pallas_call(
        functools.partial(grid_kernel, n_gx, n_gy),
        out_shape=(
            shape((5, blocks, width), f32),
            shape((n, back * cap, width), f32),
            shape((n, back * cap, width), f32),
            shape((back, 2 * slots, width), f32),
            shape((2, 2 * slots, width), f32),
        ),
        in_specs=[HBM] * 12,
        out_specs=(VMEM,) * 5,
        scratch_shapes=[
            pltpu.VMEM((depth, height, width), f32),
            pltpu.VMEM((3, depth, height, width), f32),
            pltpu.VMEM((depth, height, width), f32),
            pltpu.VMEM((slots, padding), f32),
            pltpu.VMEM((3, slots, padding), f32),
            pltpu.VMEM((slots, padding), f32),
            pltpu.VMEM((slots, padding), i32),
            pltpu.VMEM((slots, padding), i32),
            pltpu.VMEM((1, slots), i32),
            pltpu.SMEM((1, n * cap), i32),
            pltpu.SMEM((1, slots), i32),
            pltpu.SMEM((1, slots), i32),
            pltpu.SMEM((2, 2), f32),
            pltpu.VMEM((sent, slots, width), f32),
            pltpu.VMEM((n, sent * cap, width), f32),
            pltpu.VMEM((2, height, width), f32),
            pltpu.VMEM((2, height, width), f32),
            pltpu.VMEM((2, 5, depth, width), f32),
            pltpu.VMEM((2, 5, depth, width), f32),
            pltpu.VMEM((n, sent * cap, width), f32),
            pltpu.VMEM((n, back * cap, width), f32),
            pltpu.VMEM((6, height + 16, width), f32),
            pltpu.VMEM((5, height, width), f32),
            pltpu.VMEM((n, 5 * cap, width), f32),
            dma((13,)),
            dma((4,)),
            dma((4,)),
            dma((n,)),
            dma((n,)),
            dma((n,)),
            dma((n,)),
        ],
        compiler_params=pltpu.CompilerParams(
            collective_id=0, has_side_effects=True, vmem_limit_bytes=limit
        ),
        name="advance_and_couple",
    )(
        gaseous_rho,
        gaseous_flow_vector,
        gaseous_kelvin,
        sender_tile_map,
        receiver_arrival_rank.reshape(1, slots),
        bin_active_number.reshape(1, slots),
        grain_inertia,
        grain_motion_vector,
        grain_kelvin,
        grain_voxel_number,
        grain_substance_label,
        exchange_factor,
    )
    final, solid = pl.pallas_call(
        functools.partial(final_kernel, cap),
        out_shape=(shape((5, blocks, width), f32), shape((back, 2 * slots, width), f32)),
        in_specs=[SMEM] * 2 + [ANY] + [VMEM] * 4,
        out_specs=(ANY, VMEM),
        scratch_shapes=[pltpu.VMEM((5, blocks + 8, width), f32), dma((5,))],
        compiler_params=pltpu.CompilerParams(vmem_limit_bytes=limit),
        name="place_results",
    )(receiver_arrival_rank, sender_tile_map, adv, new, ret, calm, pull)
    return (
        final.reshape(5, depth, height, width),
        solid.reshape(back, slots, 2, width),
    )


def solution(mesh):
    placed = (
        P(None, "gy", "gx"),
        P(None, None, "gy", "gx"),
        P(None, "gy", "gx"),
        P(("gx", "gy"), None),
        P(("gx", "gy")),
        P(("gx", "gy")),
        P(("gx", "gy"), None),
        P(None, ("gx", "gy"), None),
        P(("gx", "gy"), None),
        P(("gx", "gy"), None),
        P(("gx", "gy"), None),
        P(),
    )
    return jax.shard_map(
        functools.partial(per_device, mesh.shape["gx"], mesh.shape["gy"]),
        mesh=mesh,
        in_specs=placed,
        out_specs=(P(None, None, "gy", "gx"), P(None, ("gx", "gy"), None, None)),
        check_vma=False,
    )
```

```python
import functools

import jax
import jax.numpy as jnp
from jax import lax
from jax.experimental import pallas as pl
from jax.experimental.pallas import tpu as pltpu
from jax.sharding import PartitionSpec as P

MESH = pl.DeviceIdType.MESH
ANY = pl.BlockSpec(memory_space=pl.ANY)
SMEM = pl.BlockSpec(memory_space=pltpu.SMEM)
step_ratio = 0.08
limit = 56 * 1024 * 1024
sent = 6
back = 4


def coefficients(ex_ref, m):
    rows = lax.broadcasted_iota(jnp.int32, (8, 128), 0)
    return jnp.where(rows < 4, ex_ref[m, 0], ex_ref[m, 1])


def bin_grains(
    rank_ref, count_ref, ex_ref, mass_ref, vel_ref, temp_ref, vox_ref, lab_ref, dense, calm_ref, pull_ref
):
    slots, padding = mass_ref.shape
    width = dense.shape[2]
    rows = lax.broadcasted_iota(jnp.int32, (8, padding), 0)
    lane = lax.broadcasted_iota(jnp.int32, (1, padding), 1)
    cells = lax.broadcasted_iota(jnp.int32, (width, padding), 0)
    factor = [coefficients(ex_ref, m) for m in range(2)]
    unroll = 8

    def body(i, carry):
        for u in range(unroll):
            k = i * unroll + u
            here = pl.ds(k, 1)
            mass = jnp.where(lane < count_ref[0, k], mass_ref[here, :], 0.0)
            base = jnp.where(rows == 4, temp_ref[here, :], 1.0)
            for c in range(3):
                base = jnp.where(rows == c + 1, vel_ref[c, here, :], base)
            base = base * mass
            label = lab_ref[here, :]
            values = jnp.concatenate(
                [jnp.where(label == 0, base, 0.0), jnp.where(label == 1, base, 0.0)], 0
            )
            onehot = jnp.where(cells == vox_ref[here, :], 1.0, 0.0).astype(jnp.bfloat16)
            total = lax.dot_general(
                jnp.concatenate(split(values, 2), 0),
                onehot,
                (((1,), (1,)), ((), ())),
                preferred_element_type=jnp.float32,
            )
            total = total[:16] + total[16:]
            pay = 0.0
            live = jnp.where(rank_ref[0, k] >= 0, 1.0, 0.0)
            for m in range(2):
                part = total[8 * m : 8 * m + 8]
                scale = 1.0 / (part[0:1] + factor[m])
                pull = factor[m] * scale
                pay = pay + pull * part
                calm = part * scale * live
                pull = pull * live
                for j in range(back):
                    calm_ref[j, pl.ds(2 * k + m, 1), :] = calm[1 + j : 2 + j]
                for j in range(2):
                    pull_ref[j, pl.ds(2 * k + m, 1), :] = pull[1 + 3 * j : 2 + 3 * j]
            for j in range(sent):
                dense[j, here, :] = pay[j : j + 1]
        return carry

    lax.fori_loop(0, slots // unroll, body, 0)


def split(x, parts):
    out = []
    for _ in range(parts):
        out.append(x.astype(jnp.bfloat16))
        x = x - out[-1].astype(jnp.float32)
    return out


def place_pay(rank_row, dense, pay_ref, cap):
    n = pay_ref.shape[0]
    slots = dense.shape[1]
    position = lax.broadcasted_iota(jnp.int32, (n * cap, slots), 0)
    onehot = jnp.where(position == rank_row[...], 1.0, 0.0).astype(jnp.bfloat16)
    onehot = jnp.concatenate([onehot] * 3, 1)
    width = dense.shape[2]
    for j in range(0, sent, 2):
        pair = [jnp.concatenate(split(dense[j + i], 3), 0) for i in range(2)]
        total = jnp.dot(onehot, jnp.concatenate(pair, 1), preferred_element_type=jnp.float32)
        for s in range(n):
            for i in range(2):
                pay_ref[s, (j + i) * cap : (j + i + 1) * cap, :] = total[
                    s * cap : (s + 1) * cap, i * width : (i + 1) * width
                ]


def face(a, b, ua, ub, wall):
    speed = 0.5 * (ua + ub) - (2.0 * step_ratio) * (b[4] - a[4]) / (a[0] + b[0])
    speed = jnp.where(wall, 0.0, speed)
    ahead = speed > 0
    return [speed * jnp.where(ahead, x, y) for x, y in zip(a, b)]


def conserve(prim):
    rho = prim[0]
    return [rho] + [rho * q for q in prim[1:]]


def grid_kernel(
    n_gx,
    n_gy,
    rho_hbm,
    vel_hbm,
    temp_hbm,
    map_hbm,
    rank_hbm,
    count_hbm,
    mass_hbm,
    motion_hbm,
    kelvin_hbm,
    vox_hbm,
    lab_hbm,
    ex_hbm,
    adv_out,
    new_out,
    ret_out,
    calm_out,
    pull_out,
    adv_ref,
    new_ref,
    calm_ref,
    pull_ref,
    rho_ref,
    vel_ref,
    temp_ref,
    mass_ref,
    motion_ref,
    kelvin_ref,
    vox_ref,
    lab_ref,
    rank_row,
    map_ref,
    rank_ref,
    count_ref,
    ex_ref,
    dense,
    pay_ref,
    xsend,
    xrecv,
    ysend,
    yrecv,
    got,
    home,
    ext,
    flux_z,
    picked,
    load_sem,
    plane_sem,
    store_sem,
    halo_send,
    halo_recv,
    pay_send,
    pay_recv,
    back_send,
    back_recv,
):
    n = n_gx * n_gy
    depth, height, width = rho_ref.shape
    cap = map_hbm.shape[1] // n
    gx = lax.axis_index("gx")
    gy = lax.axis_index("gy")
    me = gx * n_gy + gy

    def place(d):
        return (d // n_gy, lax.rem(d, n_gy))

    def ahead(k):
        x = lax.rem(gx + lax.rem(k, n_gx), n_gx)
        return x * n_gy + lax.rem(gy + k // n_gx, n_gy)

    def behind(k):
        x = lax.rem(gx + n_gx - lax.rem(k, n_gx), n_gx)
        return x * n_gy + lax.rem(gy + n_gy - k // n_gx, n_gy)

    barrier = pltpu.get_barrier_semaphore()

    def greet(k, carry):
        d = lax.rem(me + k, n)
        pl.semaphore_signal(barrier, inc=1, device_id=place(d), device_id_type=MESH)
        return carry

    loads = [
        pltpu.make_async_copy(src, dst, load_sem.at[i])
        for i, (src, dst) in enumerate(
            (
                (rank_hbm, rank_row),
                (map_hbm, map_ref),
                (rank_hbm, rank_ref),
                (count_hbm, count_ref),
                (ex_hbm, ex_ref),
                (mass_hbm, mass_ref),
                (motion_hbm, motion_ref),
                (kelvin_hbm, kelvin_ref),
                (vox_hbm, vox_ref),
                (lab_hbm, lab_ref),
                (rho_hbm, rho_ref),
                (vel_hbm, vel_ref),
                (temp_hbm, temp_ref),
            )
        )
    ]
    for load in loads:
        load.start()
    lax.fori_loop(1, n, greet, 0)
    for load in loads[:10]:
        load.wait()
    bin_grains(
        rank_ref,
        count_ref,
        ex_ref,
        mass_ref,
        motion_ref,
        kelvin_ref,
        vox_ref,
        lab_ref,
        dense,
        calm_ref,
        pull_ref,
    )
    place_pay(rank_row, dense, pay_ref, cap)

    def outward(k):
        d = ahead(k)
        return pltpu.make_async_remote_copy(
            src_ref=pay_ref.at[d],
            dst_ref=got.at[me],
            send_sem=pay_send.at[k],
            recv_sem=pay_recv.at[k],
            device_id=place(d),
            device_id_type=MESH,
        )

    def send_out(k, carry):
        outward(k).start()
        return carry

    pl.semaphore_wait(barrier, n - 1)
    early = 1 + n // 4
    lax.fori_loop(1, early, send_out, 0)
    stores = [
        pltpu.make_async_copy(src, dst, store_sem.at[i])
        for i, (src, dst) in enumerate(
            ((calm_ref, calm_out), (pull_ref, pull_out), (new_ref, new_out), (home, ret_out))
        )
    ]
    for store in stores[:2]:
        store.start()
    for load in loads[10:]:
        load.wait()

    def prim(f, z, rows):
        if f == 0:
            return rho_ref[z, rows, :]
        if f == 4:
            return temp_ref[z, rows, :]
        return vel_ref[f - 1, z, rows, :]

    whole = pl.ds(0, height)
    lanes = lax.broadcasted_iota(jnp.int32, (height, width), 1)

    def pack(z, carry):
        low, high = carry
        for f in range(5):
            spot = f * depth + z
            x = prim(f, z, whole)
            ysend[0, f, pl.ds(z, 1), :] = x[0:1]
            ysend[1, f, pl.ds(z, 1), :] = x[height - 1 : height]
            low = jnp.where(lanes == spot, pltpu.roll(x, spot, 1), low)
            high = jnp.where(lanes == spot, pltpu.roll(x, spot + 1, 1), high)
        return (low, high)

    zero = jnp.zeros((height, width), jnp.float32)
    low, high = lax.fori_loop(0, depth, pack, (zero, zero))
    xsend[0] = low
    xsend[1] = high

    def halo(which, side, device):
        src, dst = ((xsend, xrecv), (ysend, yrecv))[which]
        return pltpu.make_async_remote_copy(
            src_ref=src.at[side],
            dst_ref=dst.at[1 - side],
            send_sem=halo_send.at[2 * which + side],
            recv_sem=halo_recv.at[2 * which + 1 - side],
            device_id=device,
            device_id_type=MESH,
        )

    sides = (
        (0, 0, gx > 0, (gx - 1, gy)),
        (0, 1, gx < n_gx - 1, (gx + 1, gy)),
        (1, 0, gy > 0, (gx, gy - 1)),
        (1, 1, gy < n_gy - 1, (gx, gy + 1)),
    )
    for which, side, there, device in sides:

        @pl.when(there)
        def _(which=which, side=side, device=device):
            halo(which, side, device).start()

    lax.fori_loop(early, n, send_out, 0)

    for which, side, there, device in sides:
        recv = (xrecv, yrecv)[which]

        @pl.when(there)
        def _(which=which, side=side, device=device):
            pltpu.make_async_remote_copy(
                src_ref=(xsend, ysend)[which].at[side],
                dst_ref=(xrecv, yrecv)[which].at[side],
                send_sem=halo_send.at[2 * which + side],
                recv_sem=halo_recv.at[2 * which + side],
                device_id=device,
                device_id_type=MESH,
            ).wait()

        @pl.when(jnp.logical_not(there))
        def _(recv=recv, side=side):
            recv[side] = jnp.ones(recv.shape[1:], jnp.float32)

    west, east = gx == 0, gx == n_gx - 1
    south, north = gy == 0, gy == n_gy - 1
    flux_z[...] = jnp.zeros_like(flux_z)
    ext[...] = jnp.ones_like(ext)
    chunk = 32 if height % 32 == 0 else height
    tile = (chunk, width)
    lane = lax.broadcasted_iota(jnp.int32, tile, 1)
    row = lax.broadcasted_iota(jnp.int32, (chunk + 8, width), 0)
    first, last = lane == 0, lane == width - 1
    wall_low = jnp.logical_and(first, west)
    wall_high = jnp.logical_and(last, east)

    def plane_out(z):
        rows = pl.ds(z * height, height)
        return pltpu.make_async_copy(
            adv_ref.at[:, rows, :], adv_out.at[:, rows, :], plane_sem.at[z]
        )

    def plane(z, carry):
        above = jnp.minimum(z + 1, depth - 1)
        at_top = z == depth - 1
        here = conserve([prim(f, z, whole) for f in range(5)])
        for f in range(5):
            ext[f, 8 : 8 + height, :] = here[f]
        ext[5, 8 : 8 + height, :] = prim(2, z, whole)
        for side, at in ((0, 7), (1, 8 + height)):
            edge = [yrecv[side, f, pl.ds(z, 1), :] for f in range(5)]
            for f, q in enumerate(conserve(edge)):
                ext[f, at : at + 1, :] = q
            ext[5, at : at + 1, :] = edge[2]
        for y0 in range(0, height, chunk):
            rows = pl.ds(y0, chunk)
            own = [prim(f, z, rows) for f in range(5)]
            cons = conserve(own)
            change = [0.0] * 5
            up = [prim(f, above, rows) for f in range(5)]
            flux = face(cons, conserve(up), own[3], up[3], at_top)
            for f in range(5):
                change[f] = flux[f] - flux_z[f, rows, :]
                flux_z[f, rows, :] = flux[f]
            lower = [ext[f, pl.ds(7 + y0, chunk + 8), :] for f in range(6)]
            upper = [ext[f, pl.ds(8 + y0, chunk + 8), :] for f in range(6)]
            wall = False
            if y0 == 0:
                wall = jnp.logical_and(row == 0, south)
            if y0 + chunk == height:
                wall = jnp.logical_or(wall, jnp.logical_and(row == chunk, north))
            flux = face(lower[:5], upper[:5], lower[5], upper[5], wall)
            for f in range(5):
                change[f] = change[f] + (flux[f][1 : chunk + 1] - flux[f][:chunk])
            left, right = [], []
            for f in range(5):
                spot = f * depth + z
                left.append(
                    jnp.where(
                        first,
                        pltpu.roll(xrecv[0, rows, :], lax.rem(width - spot, width), 1),
                        pltpu.roll(own[f], 1, 1),
                    )
                )
                right.append(
                    jnp.where(
                        last,
                        pltpu.roll(xrecv[1, rows, :], width - 1 - spot, 1),
                        pltpu.roll(own[f], width - 1, 1),
                    )
                )
            flux = face(conserve(left), cons, left[1], own[1], wall_low)
            for f in range(5):
                change[f] = change[f] - flux[f]
            flux = face(cons, conserve(right), own[1], right[1], wall_high)
            for f in range(5):
                change[f] = change[f] + flux[f]
            fresh = [cons[f] - step_ratio * change[f] for f in range(5)]
            scale = 1.0 / fresh[0]
            out = pl.ds(z * height + y0, chunk)
            adv_ref[0, out, :] = fresh[0]
            for f in range(1, 5):
                adv_ref[f, out, :] = fresh[f] * scale
        plane_out(z).start()
        return carry

    lax.fori_loop(0, depth, plane, 0)

    def pick(s, carry):
        for r in range(cap):
            b = jnp.maximum(map_ref[0, s * cap + r], 0)
            for f in range(5):
                picked[s, f * cap + r : f * cap + r + 1, :] = adv_ref[f, pl.ds(b, 1), :]
        return carry

    lax.fori_loop(0, n, pick, 0)

    def part(ref, s, j):
        return ref[s, j * cap : (j + 1) * cap, :]

    def couple(ref, s):
        g = part(picked, s, 0)
        scale = 1.0 / (g + part(ref, s, 0))
        for c in range(3):
            new_ref[s, c * cap : (c + 1) * cap, :] = (
                g * part(picked, s, 1 + c) + part(ref, s, 1 + c)
            ) * scale
        new_ref[s, 3 * cap : 4 * cap, :] = (g * part(picked, s, 4) + part(ref, s, 4)) / (
            g + part(ref, s, 5)
        )

    couple(pay_ref, me)
    home[me] = new_ref[me]

    def inward(k):
        d = behind(k)
        return pltpu.make_async_remote_copy(
            src_ref=new_ref.at[d],
            dst_ref=home.at[me],
            send_sem=back_send.at[k],
            recv_sem=back_recv.at[k],
            device_id=place(d),
            device_id_type=MESH,
        )

    def answer(k, carry):
        d = behind(k)
        outward(k).wait()
        couple(got, d)
        inward(k).start()
        return carry

    lax.fori_loop(1, n, answer, 0)

    stores[2].start()

    def finish(k, carry):
        inward(k).wait()
        return carry

    lax.fori_loop(1, n, finish, 0)
    stores[3].start()
    for store in stores:
        store.wait()
    for z in range(depth):
        plane_out(z).wait()


def final_kernel(
    cap,
    rank_ref,
    map_ref,
    adv_ref,
    new_hbm,
    ret_hbm,
    calm_hbm,
    pull_hbm,
    out_ref,
    solid_out,
    held,
    new_ref,
    ret_ref,
    calm_ref,
    pull_ref,
    solid_ref,
    load_sem,
    store_sem,
):
    slots = rank_ref.shape[0]
    positions = map_ref.shape[1]
    fields, blocks, width = adv_ref.shape

    def rows(f):
        return held.at[f, pl.ds(0, blocks), :]

    loads = [
        pltpu.make_async_copy(src, dst, load_sem.at[i])
        for i, (src, dst) in enumerate(
            [(new_hbm, new_ref)]
            + [(adv_ref.at[f], rows(f)) for f in range(fields)]
            + [(ret_hbm, ret_ref), (calm_hbm, calm_ref), (pull_hbm, pull_ref)]
        )
    ]
    stores = [
        pltpu.make_async_copy(src, dst, store_sem.at[i])
        for i, (src, dst) in enumerate(
            [(rows(f), out_ref.at[f]) for f in range(fields)] + [(solid_ref, solid_out)]
        )
    ]
    for load in loads:
        load.start()
    for load in loads[: fields + 1]:
        load.wait()
    stores[0].start()

    def scatter(i, carry):
        for u in range(cap):
            b = map_ref[0, i * cap + u]
            b = jnp.where(b >= 0, b, blocks)
            for j in range(back):
                held[1 + j, pl.ds(b, 1), :] = new_ref[i, j * cap + u : j * cap + u + 1, :]
        return carry

    lax.fori_loop(0, positions // cap, scatter, 0)
    for f in range(1, fields):
        stores[f].start()
    for load in loads[fields + 1 :]:
        load.wait()
    unroll = 8

    def solid(i, carry):
        for u in range(unroll):
            k = i * unroll + u
            v = jnp.maximum(rank_ref[k], 0)
            s = v // cap
            r = v % cap
            for j in range(back):
                row = ret_ref[s, pl.ds(j * cap + r, 1), :]
                solid_ref[j, pl.ds(2 * k, 2), :] = jnp.broadcast_to(row, (2, width))
        return carry

    lax.fori_loop(0, slots // unroll, solid, 0)
    for j in range(back):
        solid_ref[j] = calm_ref[j] + pull_ref[j // 3] * solid_ref[j]
    stores[fields].start()
    for store in stores:
        store.wait()


def per_device(
    n_gx,
    n_gy,
    gaseous_rho,
    gaseous_flow_vector,
    gaseous_kelvin,
    sender_tile_map,
    receiver_arrival_rank,
    bin_active_number,
    grain_inertia,
    grain_motion_vector,
    grain_kelvin,
    grain_voxel_number,
    grain_substance_label,
    exchange_factor,
):
    n = n_gx * n_gy
    depth, height, width = gaseous_rho.shape
    slots, padding = grain_inertia.shape
    cap = sender_tile_map.shape[1] // n
    blocks = depth * height
    f32, i32 = jnp.float32, jnp.int32
    shape = jax.ShapeDtypeStruct
    dma = pltpu.SemaphoreType.DMA
    adv, new, ret, calm, pull = pl.pallas_call(
        functools.partial(grid_kernel, n_gx, n_gy),
        out_shape=(
            shape((5, blocks, width), f32),
            shape((n, back * cap, width), f32),
            shape((n, back * cap, width), f32),
            shape((back, 2 * slots, width), f32),
            shape((2, 2 * slots, width), f32),
        ),
        in_specs=[ANY] * 12,
        out_specs=(ANY,) * 5,
        scratch_shapes=[
            pltpu.VMEM((5, blocks, width), f32),
            pltpu.VMEM((n, back * cap, width), f32),
            pltpu.VMEM((back, 2 * slots, width), f32),
            pltpu.VMEM((2, 2 * slots, width), f32),
            pltpu.VMEM((depth, height, width), f32),
            pltpu.VMEM((3, depth, height, width), f32),
            pltpu.VMEM((depth, height, width), f32),
            pltpu.VMEM((slots, padding), f32),
            pltpu.VMEM((3, slots, padding), f32),
            pltpu.VMEM((slots, padding), f32),
            pltpu.VMEM((slots, padding), i32),
            pltpu.VMEM((slots, padding), i32),
            pltpu.VMEM((1, slots), i32),
            pltpu.SMEM((1, n * cap), i32),
            pltpu.SMEM((1, slots), i32),
            pltpu.SMEM((1, slots), i32),
            pltpu.SMEM((2, 2), f32),
            pltpu.VMEM((sent, slots, width), f32),
            pltpu.VMEM((n, sent * cap, width), f32),
            pltpu.VMEM((2, height, width), f32),
            pltpu.VMEM((2, height, width), f32),
            pltpu.VMEM((2, 5, depth, width), f32),
            pltpu.VMEM((2, 5, depth, width), f32),
            pltpu.VMEM((n, sent * cap, width), f32),
            pltpu.VMEM((n, back * cap, width), f32),
            pltpu.VMEM((6, height + 16, width), f32),
            pltpu.VMEM((5, height, width), f32),
            pltpu.VMEM((n, 5 * cap, width), f32),
            dma((13,)),
            dma((depth,)),
            dma((4,)),
            dma((4,)),
            dma((4,)),
            dma((n,)),
            dma((n,)),
            dma((n,)),
            dma((n,)),
        ],
        compiler_params=pltpu.CompilerParams(
            collective_id=0, has_side_effects=True, vmem_limit_bytes=limit
        ),
        name="advance_and_couple",
    )(
        gaseous_rho,
        gaseous_flow_vector,
        gaseous_kelvin,
        sender_tile_map,
        receiver_arrival_rank.reshape(1, slots),
        bin_active_number.reshape(1, slots),
        grain_inertia,
        grain_motion_vector,
        grain_kelvin,
        grain_voxel_number,
        grain_substance_label,
        exchange_factor,
    )
    final, solid = pl.pallas_call(
        functools.partial(final_kernel, cap),
        out_shape=(shape((5, blocks, width), f32), shape((back, 2 * slots, width), f32)),
        in_specs=[SMEM] * 2 + [ANY] * 5,
        out_specs=(ANY, ANY),
        scratch_shapes=[
            pltpu.VMEM((5, blocks + 8, width), f32),
            pltpu.VMEM((n, back * cap, width), f32),
            pltpu.VMEM((n, back * cap, width), f32),
            pltpu.VMEM((back, 2 * slots, width), f32),
            pltpu.VMEM((2, 2 * slots, width), f32),
            pltpu.VMEM((back, 2 * slots, width), f32),
            dma((9,)),
            dma((6,)),
        ],
        compiler_params=pltpu.CompilerParams(vmem_limit_bytes=limit),
        name="place_results",
    )(receiver_arrival_rank, sender_tile_map, adv, new, ret, calm, pull)
    return (
        final.reshape(5, depth, height, width),
        solid.reshape(back, slots, 2, width),
    )


def solution(mesh):
    placed = (
        P(None, "gy", "gx"),
        P(None, None, "gy", "gx"),
        P(None, "gy", "gx"),
        P(("gx", "gy"), None),
        P(("gx", "gy")),
        P(("gx", "gy")),
        P(("gx", "gy"), None),
        P(None, ("gx", "gy"), None),
        P(("gx", "gy"), None),
        P(("gx", "gy"), None),
        P(("gx", "gy"), None),
        P(),
    )
    return jax.shard_map(
        functools.partial(per_device, mesh.shape["gx"], mesh.shape["gy"]),
        mesh=mesh,
        in_specs=placed,
        out_specs=(P(None, None, "gy", "gx"), P(None, ("gx", "gy"), None, None)),
        check_vma=False,
    )
```

```python
import functools

import jax
import jax.numpy as jnp
from jax import lax
from jax.experimental import pallas as pl
from jax.experimental.pallas import tpu as pltpu
from jax.sharding import PartitionSpec as P

MESH = pl.DeviceIdType.MESH
ANY = pl.BlockSpec(memory_space=pl.ANY)
SMEM = pl.BlockSpec(memory_space=pltpu.SMEM)
step_ratio = 0.08
limit = 56 * 1024 * 1024
sent = 6
back = 4


def coefficients(ex_ref, m):
    rows = lax.broadcasted_iota(jnp.int32, (8, 128), 0)
    return jnp.where(rows < 4, ex_ref[m, 0], ex_ref[m, 1])


def bin_grains(
    rank_ref, count_ref, ex_ref, mass_ref, vel_ref, temp_ref, vox_ref, lab_ref, dense, calm_ref, pull_ref
):
    slots, padding = mass_ref.shape
    width = dense.shape[2]
    rows = lax.broadcasted_iota(jnp.int32, (8, padding), 0)
    lane = lax.broadcasted_iota(jnp.int32, (1, padding), 1)
    cells = lax.broadcasted_iota(jnp.int32, (width, padding), 0)
    factor = [coefficients(ex_ref, m) for m in range(2)]
    unroll = 8

    def body(i, carry):
        for u in range(unroll):
            k = i * unroll + u
            here = pl.ds(k, 1)
            mass = jnp.where(lane < count_ref[0, k], mass_ref[here, :], 0.0)
            base = jnp.where(rows == 4, temp_ref[here, :], 1.0)
            for c in range(3):
                base = jnp.where(rows == c + 1, vel_ref[c, here, :], base)
            base = base * mass
            label = lab_ref[here, :]
            values = jnp.concatenate(
                [jnp.where(label == 0, base, 0.0), jnp.where(label == 1, base, 0.0)], 0
            )
            onehot = jnp.where(cells == vox_ref[here, :], 1.0, 0.0).astype(jnp.bfloat16)
            total = lax.dot_general(
                jnp.concatenate(split(values, 2), 0),
                onehot,
                (((1,), (1,)), ((), ())),
                preferred_element_type=jnp.float32,
            )
            total = total[:16] + total[16:]
            pay = 0.0
            live = jnp.where(rank_ref[0, k] >= 0, 1.0, 0.0)
            for m in range(2):
                part = total[8 * m : 8 * m + 8]
                scale = 1.0 / (part[0:1] + factor[m])
                pull = factor[m] * scale
                pay = pay + pull * part
                calm = part * scale * live
                pull = pull * live
                for j in range(back):
                    calm_ref[j, pl.ds(2 * k + m, 1), :] = calm[1 + j : 2 + j]
                for j in range(2):
                    pull_ref[j, pl.ds(2 * k + m, 1), :] = pull[1 + 3 * j : 2 + 3 * j]
            for j in range(sent):
                dense[j, here, :] = pay[j : j + 1]
        return carry

    lax.fori_loop(0, slots // unroll, body, 0)


def split(x, parts):
    out = []
    for _ in range(parts):
        out.append(x.astype(jnp.bfloat16))
        x = x - out[-1].astype(jnp.float32)
    return out


def place_pay(rank_row, dense, pay_ref, cap):
    n = pay_ref.shape[0]
    slots = dense.shape[1]
    position = lax.broadcasted_iota(jnp.int32, (n * cap, slots), 0)
    onehot = jnp.where(position == rank_row[...], 1.0, 0.0).astype(jnp.bfloat16)
    onehot = jnp.concatenate([onehot] * 3, 1)
    width = dense.shape[2]
    for j in range(0, sent, 2):
        pair = [jnp.concatenate(split(dense[j + i], 3), 0) for i in range(2)]
        total = jnp.dot(onehot, jnp.concatenate(pair, 1), preferred_element_type=jnp.float32)
        for s in range(n):
            for i in range(2):
                pay_ref[s, (j + i) * cap : (j + i + 1) * cap, :] = total[
                    s * cap : (s + 1) * cap, i * width : (i + 1) * width
                ]


def face(a, b, ua, ub, wall):
    speed = 0.5 * (ua + ub) - (2.0 * step_ratio) * (b[4] - a[4]) / (a[0] + b[0])
    speed = jnp.where(wall, 0.0, speed)
    ahead = speed > 0
    return [speed * jnp.where(ahead, x, y) for x, y in zip(a, b)]


def conserve(prim):
    rho = prim[0]
    return [rho] + [rho * q for q in prim[1:]]


def grid_kernel(
    n_gx,
    n_gy,
    rho_hbm,
    vel_hbm,
    temp_hbm,
    map_hbm,
    rank_hbm,
    count_hbm,
    mass_hbm,
    motion_hbm,
    kelvin_hbm,
    vox_hbm,
    lab_hbm,
    ex_hbm,
    adv_out,
    ret_out,
    calm_out,
    pull_out,
    adv_ref,
    fin_ref,
    index_row,
    index_ref,
    new_ref,
    calm_ref,
    pull_ref,
    rho_ref,
    vel_ref,
    temp_ref,
    mass_ref,
    motion_ref,
    kelvin_ref,
    vox_ref,
    lab_ref,
    rank_row,
    map_ref,
    rank_ref,
    count_ref,
    ex_ref,
    dense,
    pay_ref,
    xsend,
    xrecv,
    ysend,
    yrecv,
    got,
    home,
    ext,
    flux_z,
    picked,
    load_sem,
    plane_sem,
    final_sem,
    index_sem,
    store_sem,
    halo_send,
    halo_recv,
    pay_send,
    pay_recv,
    back_send,
    back_recv,
):
    n = n_gx * n_gy
    depth, height, width = rho_ref.shape
    cap = map_hbm.shape[1] // n
    gx = lax.axis_index("gx")
    gy = lax.axis_index("gy")
    me = gx * n_gy + gy

    def place(d):
        return (d // n_gy, lax.rem(d, n_gy))

    def ahead(k):
        x = lax.rem(gx + lax.rem(k, n_gx), n_gx)
        return x * n_gy + lax.rem(gy + k // n_gx, n_gy)

    def behind(k):
        x = lax.rem(gx + n_gx - lax.rem(k, n_gx), n_gx)
        return x * n_gy + lax.rem(gy + n_gy - k // n_gx, n_gy)

    barrier = pltpu.get_barrier_semaphore()

    def greet(k, carry):
        d = lax.rem(me + k, n)
        pl.semaphore_signal(barrier, inc=1, device_id=place(d), device_id_type=MESH)
        return carry

    loads = [
        pltpu.make_async_copy(src, dst, load_sem.at[i])
        for i, (src, dst) in enumerate(
            (
                (rank_hbm, rank_row),
                (map_hbm, map_ref),
                (rank_hbm, rank_ref),
                (count_hbm, count_ref),
                (ex_hbm, ex_ref),
                (mass_hbm, mass_ref),
                (motion_hbm, motion_ref),
                (kelvin_hbm, kelvin_ref),
                (vox_hbm, vox_ref),
                (lab_hbm, lab_ref),
                (rho_hbm, rho_ref),
                (vel_hbm, vel_ref),
                (temp_hbm, temp_ref),
            )
        )
    ]
    for load in loads:
        load.start()
    lax.fori_loop(1, n, greet, 0)
    for load in loads[:10]:
        load.wait()
    bin_grains(
        rank_ref,
        count_ref,
        ex_ref,
        mass_ref,
        motion_ref,
        kelvin_ref,
        vox_ref,
        lab_ref,
        dense,
        calm_ref,
        pull_ref,
    )
    place_pay(rank_row, dense, pay_ref, cap)

    def outward(k):
        d = ahead(k)
        return pltpu.make_async_remote_copy(
            src_ref=pay_ref.at[d],
            dst_ref=got.at[me],
            send_sem=pay_send.at[k],
            recv_sem=pay_recv.at[k],
            device_id=place(d),
            device_id_type=MESH,
        )

    def send_out(k, carry):
        outward(k).start()
        return carry

    pl.semaphore_wait(barrier, n - 1)
    early = 1 + n // 4
    lax.fori_loop(1, early, send_out, 0)
    stores = [
        pltpu.make_async_copy(src, dst, store_sem.at[i])
        for i, (src, dst) in enumerate(
            ((calm_ref, calm_out), (pull_ref, pull_out), (home, ret_out))
        )
    ]
    for store in stores[:2]:
        store.start()
    for load in loads[10:]:
        load.wait()

    def prim(f, z, rows):
        if f == 0:
            return rho_ref[z, rows, :]
        if f == 4:
            return temp_ref[z, rows, :]
        return vel_ref[f - 1, z, rows, :]

    whole = pl.ds(0, height)
    lanes = lax.broadcasted_iota(jnp.int32, (height, width), 1)

    def pack(z, carry):
        low, high = carry
        for f in range(5):
            spot = f * depth + z
            x = prim(f, z, whole)
            ysend[0, f, pl.ds(z, 1), :] = x[0:1]
            ysend[1, f, pl.ds(z, 1), :] = x[height - 1 : height]
            low = jnp.where(lanes == spot, pltpu.roll(x, spot, 1), low)
            high = jnp.where(lanes == spot, pltpu.roll(x, spot + 1, 1), high)
        return (low, high)

    zero = jnp.zeros((height, width), jnp.float32)
    low, high = lax.fori_loop(0, depth, pack, (zero, zero))
    xsend[0] = low
    xsend[1] = high

    def halo(which, side, device):
        src, dst = ((xsend, xrecv), (ysend, yrecv))[which]
        return pltpu.make_async_remote_copy(
            src_ref=src.at[side],
            dst_ref=dst.at[1 - side],
            send_sem=halo_send.at[2 * which + side],
            recv_sem=halo_recv.at[2 * which + 1 - side],
            device_id=device,
            device_id_type=MESH,
        )

    sides = (
        (0, 0, gx > 0, (gx - 1, gy)),
        (0, 1, gx < n_gx - 1, (gx + 1, gy)),
        (1, 0, gy > 0, (gx, gy - 1)),
        (1, 1, gy < n_gy - 1, (gx, gy + 1)),
    )
    for which, side, there, device in sides:

        @pl.when(there)
        def _(which=which, side=side, device=device):
            halo(which, side, device).start()

    lax.fori_loop(early, n, send_out, 0)

    blocks = depth * height
    number = lax.broadcasted_iota(jnp.int32, index_row.shape, 0) * width
    number = number + lax.broadcasted_iota(jnp.int32, index_row.shape, 1)

    def mark(s, index):
        for r in range(cap):
            i = s * cap + r
            index = jnp.where(number == map_ref[0, i], blocks + i, index)
        return index

    index_row[...] = lax.fori_loop(0, n, mark, number)
    index_copy = pltpu.make_async_copy(index_row, index_ref, index_sem)
    index_copy.start()

    for which, side, there, device in sides:
        recv = (xrecv, yrecv)[which]

        @pl.when(there)
        def _(which=which, side=side, device=device):
            pltpu.make_async_remote_copy(
                src_ref=(xsend, ysend)[which].at[side],
                dst_ref=(xrecv, yrecv)[which].at[side],
                send_sem=halo_send.at[2 * which + side],
                recv_sem=halo_recv.at[2 * which + side],
                device_id=device,
                device_id_type=MESH,
            ).wait()

        @pl.when(jnp.logical_not(there))
        def _(recv=recv, side=side):
            recv[side] = jnp.ones(recv.shape[1:], jnp.float32)

    west, east = gx == 0, gx == n_gx - 1
    south, north = gy == 0, gy == n_gy - 1
    flux_z[...] = jnp.zeros_like(flux_z)
    ext[...] = jnp.ones_like(ext)
    chunk = 32 if height % 32 == 0 else height
    tile = (chunk, width)
    lane = lax.broadcasted_iota(jnp.int32, tile, 1)
    row = lax.broadcasted_iota(jnp.int32, (chunk + 8, width), 0)
    first, last = lane == 0, lane == width - 1
    wall_low = jnp.logical_and(first, west)
    wall_high = jnp.logical_and(last, east)

    def plane_out(z):
        rows = pl.ds(z * height, height)
        return pltpu.make_async_copy(
            adv_ref.at[0, rows, :], adv_out.at[0, rows, :], plane_sem.at[z]
        )

    def final_out(z):
        rows = pl.ds(z * height, height)
        return pltpu.make_async_copy(
            fin_ref.at[:, rows, :], adv_out.at[pl.ds(1, back), rows, :], final_sem.at[z]
        )

    def plane(z, carry):
        above = jnp.minimum(z + 1, depth - 1)
        at_top = z == depth - 1
        here = conserve([prim(f, z, whole) for f in range(5)])
        for f in range(5):
            ext[f, 8 : 8 + height, :] = here[f]
        ext[5, 8 : 8 + height, :] = prim(2, z, whole)
        for side, at in ((0, 7), (1, 8 + height)):
            edge = [yrecv[side, f, pl.ds(z, 1), :] for f in range(5)]
            for f, q in enumerate(conserve(edge)):
                ext[f, at : at + 1, :] = q
            ext[5, at : at + 1, :] = edge[2]
        for y0 in range(0, height, chunk):
            rows = pl.ds(y0, chunk)
            own = [prim(f, z, rows) for f in range(5)]
            cons = conserve(own)
            change = [0.0] * 5
            up = [prim(f, above, rows) for f in range(5)]
            flux = face(cons, conserve(up), own[3], up[3], at_top)
            for f in range(5):
                change[f] = flux[f] - flux_z[f, rows, :]
                flux_z[f, rows, :] = flux[f]
            lower = [ext[f, pl.ds(7 + y0, chunk + 8), :] for f in range(6)]
            upper = [ext[f, pl.ds(8 + y0, chunk + 8), :] for f in range(6)]
            wall = False
            if y0 == 0:
                wall = jnp.logical_and(row == 0, south)
            if y0 + chunk == height:
                wall = jnp.logical_or(wall, jnp.logical_and(row == chunk, north))
            flux = face(lower[:5], upper[:5], lower[5], upper[5], wall)
            for f in range(5):
                change[f] = change[f] + (flux[f][1 : chunk + 1] - flux[f][:chunk])
            left, right = [], []
            for f in range(5):
                spot = f * depth + z
                left.append(
                    jnp.where(
                        first,
                        pltpu.roll(xrecv[0, rows, :], lax.rem(width - spot, width), 1),
                        pltpu.roll(own[f], 1, 1),
                    )
                )
                right.append(
                    jnp.where(
                        last,
                        pltpu.roll(xrecv[1, rows, :], width - 1 - spot, 1),
                        pltpu.roll(own[f], width - 1, 1),
                    )
                )
            flux = face(conserve(left), cons, left[1], own[1], wall_low)
            for f in range(5):
                change[f] = change[f] - flux[f]
            flux = face(cons, conserve(right), own[1], right[1], wall_high)
            for f in range(5):
                change[f] = change[f] + flux[f]
            fresh = [cons[f] - step_ratio * change[f] for f in range(5)]
            scale = 1.0 / fresh[0]
            out = pl.ds(z * height + y0, chunk)
            adv_ref[0, out, :] = fresh[0]
            for f in range(1, 5):
                adv_ref[f, out, :] = fresh[f] * scale
        plane_out(z).start()
        return carry

    lax.fori_loop(0, depth, plane, 0)

    def pick(s, carry):
        for r in range(cap):
            b = jnp.maximum(map_ref[0, s * cap + r], 0)
            for f in range(5):
                picked[s, f * cap + r : f * cap + r + 1, :] = adv_ref[f, pl.ds(b, 1), :]
        return carry

    lax.fori_loop(0, n, pick, 0)

    def part(ref, s, j):
        return ref[s, j * cap : (j + 1) * cap, :]

    def couple(ref, s):
        g = part(picked, s, 0)
        scale = 1.0 / (g + part(ref, s, 0))
        fresh = [(g * part(picked, s, 1 + c) + part(ref, s, 1 + c)) * scale for c in range(3)]
        fresh.append((g * part(picked, s, 4) + part(ref, s, 4)) / (g + part(ref, s, 5)))
        for j in range(back):
            new_ref[s, j * cap : (j + 1) * cap, :] = fresh[j]
            adv_ref[1 + j, pl.ds(blocks + s * cap, cap), :] = fresh[j]

    couple(pay_ref, me)
    home[me] = new_ref[me]

    def inward(k):
        d = behind(k)
        return pltpu.make_async_remote_copy(
            src_ref=new_ref.at[d],
            dst_ref=home.at[me],
            send_sem=back_send.at[k],
            recv_sem=back_recv.at[k],
            device_id=place(d),
            device_id_type=MESH,
        )

    def answer(k, carry):
        d = behind(k)
        outward(k).wait()
        couple(got, d)
        inward(k).start()
        return carry

    lax.fori_loop(1, n, answer, 0)

    index_copy.wait()
    unroll = 8

    def assemble(z, carry):
        def some(i, carry):
            for u in range(unroll):
                b = z * height + i * unroll + u
                source = index_ref[b // width, lax.rem(b, width)]
                for j in range(back):
                    fin_ref[j, pl.ds(b, 1), :] = adv_ref[1 + j, pl.ds(source, 1), :]
            return carry

        lax.fori_loop(0, height // unroll, some, 0)
        final_out(z).start()
        return carry

    lax.fori_loop(0, depth, assemble, 0)

    def finish(k, carry):
        inward(k).wait()
        return carry

    lax.fori_loop(1, n, finish, 0)
    stores[2].start()
    for store in stores:
        store.wait()
    for z in range(depth):
        plane_out(z).wait()
        final_out(z).wait()


def final_kernel(
    cap,
    rank_ref,
    adv_ref,
    ret_hbm,
    calm_hbm,
    pull_hbm,
    out_ref,
    solid_out,
    ret_ref,
    calm_ref,
    pull_ref,
    solid_ref,
    load_sem,
    store_sem,
):
    slots = rank_ref.shape[0]
    fields, blocks, width = adv_ref.shape
    loads = [
        pltpu.make_async_copy(src, dst, load_sem.at[i])
        for i, (src, dst) in enumerate(
            ((ret_hbm, ret_ref), (calm_hbm, calm_ref), (pull_hbm, pull_ref))
        )
    ]
    stores = [
        pltpu.make_async_copy(src, dst, store_sem.at[i])
        for i, (src, dst) in enumerate(
            [(adv_ref.at[f], out_ref.at[f]) for f in range(fields)] + [(solid_ref, solid_out)]
        )
    ]
    for load in loads:
        load.start()
    for store in stores[:fields]:
        store.start()
    for load in loads:
        load.wait()
    unroll = 8

    def solid(i, carry):
        for u in range(unroll):
            k = i * unroll + u
            v = jnp.maximum(rank_ref[k], 0)
            s = v // cap
            r = v % cap
            for j in range(back):
                row = ret_ref[s, pl.ds(j * cap + r, 1), :]
                solid_ref[j, pl.ds(2 * k, 2), :] = jnp.broadcast_to(row, (2, width))
        return carry

    lax.fori_loop(0, slots // unroll, solid, 0)
    for j in range(back):
        solid_ref[j] = calm_ref[j] + pull_ref[j // 3] * solid_ref[j]
    stores[fields].start()
    for store in stores:
        store.wait()


def per_device(
    n_gx,
    n_gy,
    gaseous_rho,
    gaseous_flow_vector,
    gaseous_kelvin,
    sender_tile_map,
    receiver_arrival_rank,
    bin_active_number,
    grain_inertia,
    grain_motion_vector,
    grain_kelvin,
    grain_voxel_number,
    grain_substance_label,
    exchange_factor,
):
    n = n_gx * n_gy
    depth, height, width = gaseous_rho.shape
    slots, padding = grain_inertia.shape
    cap = sender_tile_map.shape[1] // n
    blocks = depth * height
    f32, i32 = jnp.float32, jnp.int32
    shape = jax.ShapeDtypeStruct
    dma = pltpu.SemaphoreType.DMA
    adv, ret, calm, pull = pl.pallas_call(
        functools.partial(grid_kernel, n_gx, n_gy),
        out_shape=(
            shape((5, blocks, width), f32),
            shape((n, back * cap, width), f32),
            shape((back, 2 * slots, width), f32),
            shape((2, 2 * slots, width), f32),
        ),
        in_specs=[ANY] * 12,
        out_specs=(ANY,) * 4,
        scratch_shapes=[
            pltpu.VMEM((5, blocks + n * cap, width), f32),
            pltpu.VMEM((back, blocks, width), f32),
            pltpu.VMEM((blocks // width, width), i32),
            pltpu.SMEM((blocks // width, width), i32),
            pltpu.VMEM((n, back * cap, width), f32),
            pltpu.VMEM((back, 2 * slots, width), f32),
            pltpu.VMEM((2, 2 * slots, width), f32),
            pltpu.VMEM((depth, height, width), f32),
            pltpu.VMEM((3, depth, height, width), f32),
            pltpu.VMEM((depth, height, width), f32),
            pltpu.VMEM((slots, padding), f32),
            pltpu.VMEM((3, slots, padding), f32),
            pltpu.VMEM((slots, padding), f32),
            pltpu.VMEM((slots, padding), i32),
            pltpu.VMEM((slots, padding), i32),
            pltpu.VMEM((1, slots), i32),
            pltpu.SMEM((1, n * cap), i32),
            pltpu.SMEM((1, slots), i32),
            pltpu.SMEM((1, slots), i32),
            pltpu.SMEM((2, 2), f32),
            pltpu.VMEM((sent, slots, width), f32),
            pltpu.VMEM((n, sent * cap, width), f32),
            pltpu.VMEM((2, height, width), f32),
            pltpu.VMEM((2, height, width), f32),
            pltpu.VMEM((2, 5, depth, width), f32),
            pltpu.VMEM((2, 5, depth, width), f32),
            pltpu.VMEM((n, sent * cap, width), f32),
            pltpu.VMEM((n, back * cap, width), f32),
            pltpu.VMEM((6, height + 16, width), f32),
            pltpu.VMEM((5, height, width), f32),
            pltpu.VMEM((n, 5 * cap, width), f32),
            dma((13,)),
            dma((depth,)),
            dma((depth,)),
            dma,
            dma((3,)),
            dma((4,)),
            dma((4,)),
            dma((n,)),
            dma((n,)),
            dma((n,)),
            dma((n,)),
        ],
        compiler_params=pltpu.CompilerParams(
            collective_id=0, has_side_effects=True, vmem_limit_bytes=limit
        ),
        name="advance_and_couple",
    )(
        gaseous_rho,
        gaseous_flow_vector,
        gaseous_kelvin,
        sender_tile_map,
        receiver_arrival_rank.reshape(1, slots),
        bin_active_number.reshape(1, slots),
        grain_inertia,
        grain_motion_vector,
        grain_kelvin,
        grain_voxel_number,
        grain_substance_label,
        exchange_factor,
    )
    final, solid = pl.pallas_call(
        functools.partial(final_kernel, cap),
        out_shape=(shape((5, blocks, width), f32), shape((back, 2 * slots, width), f32)),
        in_specs=[SMEM] + [ANY] * 4,
        out_specs=(ANY, ANY),
        scratch_shapes=[
            pltpu.VMEM((n, back * cap, width), f32),
            pltpu.VMEM((back, 2 * slots, width), f32),
            pltpu.VMEM((2, 2 * slots, width), f32),
            pltpu.VMEM((back, 2 * slots, width), f32),
            dma((3,)),
            dma((6,)),
        ],
        compiler_params=pltpu.CompilerParams(vmem_limit_bytes=limit),
        name="place_results",
    )(receiver_arrival_rank, adv, ret, calm, pull)
    return (
        final.reshape(5, depth, height, width),
        solid.reshape(back, slots, 2, width),
    )


def solution(mesh):
    placed = (
        P(None, "gy", "gx"),
        P(None, None, "gy", "gx"),
        P(None, "gy", "gx"),
        P(("gx", "gy"), None),
        P(("gx", "gy")),
        P(("gx", "gy")),
        P(("gx", "gy"), None),
        P(None, ("gx", "gy"), None),
        P(("gx", "gy"), None),
        P(("gx", "gy"), None),
        P(("gx", "gy"), None),
        P(),
    )
    return jax.shard_map(
        functools.partial(per_device, mesh.shape["gx"], mesh.shape["gy"]),
        mesh=mesh,
        in_specs=placed,
        out_specs=(P(None, None, "gy", "gx"), P(None, ("gx", "gy"), None, None)),
        check_vma=False,
    )
```

```python
import functools

import jax
import jax.numpy as jnp
from jax import lax
from jax.experimental import pallas as pl
from jax.experimental.pallas import tpu as pltpu
from jax.sharding import PartitionSpec as P

MESH = pl.DeviceIdType.MESH
ANY = pl.BlockSpec(memory_space=pl.ANY)
SMEM = pl.BlockSpec(memory_space=pltpu.SMEM)
step_ratio = 0.08
limit = 56 * 1024 * 1024
sent = 6
back = 4


def coefficients(ex_ref, m):
    rows = lax.broadcasted_iota(jnp.int32, (8, 128), 0)
    return jnp.where(rows < 4, ex_ref[m, 0], ex_ref[m, 1])


def bin_grains(
    rank_ref, count_ref, ex_ref, mass_ref, vel_ref, temp_ref, vox_ref, lab_ref, dense, calm_ref, pull_ref
):
    slots, padding = mass_ref.shape
    width = dense.shape[2]
    rows = lax.broadcasted_iota(jnp.int32, (8, padding), 0)
    lane = lax.broadcasted_iota(jnp.int32, (1, padding), 1)
    cells = lax.broadcasted_iota(jnp.int32, (width, padding), 0)
    factor = [coefficients(ex_ref, m) for m in range(2)]
    unroll = 8

    def body(i, carry):
        for u in range(unroll):
            k = i * unroll + u
            here = pl.ds(k, 1)
            mass = jnp.where(lane < count_ref[0, k], mass_ref[here, :], 0.0)
            base = jnp.where(rows == 4, temp_ref[here, :], 1.0)
            for c in range(3):
                base = jnp.where(rows == c + 1, vel_ref[c, here, :], base)
            base = base * mass
            label = lab_ref[here, :]
            values = jnp.concatenate(
                [jnp.where(label == 0, base, 0.0), jnp.where(label == 1, base, 0.0)], 0
            )
            onehot = jnp.where(cells == vox_ref[here, :], 1.0, 0.0).astype(jnp.bfloat16)
            total = lax.dot_general(
                jnp.concatenate(split(values, 2), 0),
                onehot,
                (((1,), (1,)), ((), ())),
                preferred_element_type=jnp.float32,
            )
            total = total[:16] + total[16:]
            pay = 0.0
            live = jnp.where(rank_ref[0, k] >= 0, 1.0, 0.0)
            for m in range(2):
                part = total[8 * m : 8 * m + 8]
                scale = 1.0 / (part[0:1] + factor[m])
                pull = factor[m] * scale
                pay = pay + pull * part
                calm = part * scale * live
                pull = pull * live
                for j in range(back):
                    calm_ref[j, pl.ds(2 * k + m, 1), :] = calm[1 + j : 2 + j]
                for j in range(2):
                    pull_ref[j, pl.ds(2 * k + m, 1), :] = pull[1 + 3 * j : 2 + 3 * j]
            for j in range(sent):
                dense[j, here, :] = pay[j : j + 1]
        return carry

    lax.fori_loop(0, slots // unroll, body, 0)


def split(x, parts):
    out = []
    for _ in range(parts):
        out.append(x.astype(jnp.bfloat16))
        x = x - out[-1].astype(jnp.float32)
    return out


def place_pay(rank_row, dense, pay_ref, cap):
    n = pay_ref.shape[0]
    slots = dense.shape[1]
    position = lax.broadcasted_iota(jnp.int32, (n * cap, slots), 0)
    onehot = jnp.where(position == rank_row[...], 1.0, 0.0).astype(jnp.bfloat16)
    onehot = jnp.concatenate([onehot] * 3, 1)
    width = dense.shape[2]
    for j in range(0, sent, 2):
        pair = [jnp.concatenate(split(dense[j + i], 3), 0) for i in range(2)]
        total = jnp.dot(onehot, jnp.concatenate(pair, 1), preferred_element_type=jnp.float32)
        for s in range(n):
            for i in range(2):
                pay_ref[s, (j + i) * cap : (j + i + 1) * cap, :] = total[
                    s * cap : (s + 1) * cap, i * width : (i + 1) * width
                ]


def face(a, b, ua, ub, wall):
    speed = 0.5 * (ua + ub) - (2.0 * step_ratio) * (b[4] - a[4]) / (a[0] + b[0])
    speed = jnp.where(wall, 0.0, speed)
    ahead = speed > 0
    return [speed * jnp.where(ahead, x, y) for x, y in zip(a, b)]


def conserve(prim):
    rho = prim[0]
    return [rho] + [rho * q for q in prim[1:]]


def grid_kernel(
    n_gx,
    n_gy,
    rho_hbm,
    vel_hbm,
    temp_hbm,
    map_hbm,
    rank_hbm,
    count_hbm,
    mass_hbm,
    motion_hbm,
    kelvin_hbm,
    vox_hbm,
    lab_hbm,
    ex_hbm,
    adv_out,
    ret_out,
    calm_out,
    pull_out,
    adv_ref,
    fin_ref,
    index_row,
    index_ref,
    new_ref,
    calm_ref,
    pull_ref,
    rho_ref,
    vel_ref,
    temp_ref,
    mass_ref,
    motion_ref,
    kelvin_ref,
    vox_ref,
    lab_ref,
    rank_row,
    map_ref,
    rank_ref,
    count_ref,
    ex_ref,
    dense,
    pay_ref,
    xsend,
    xrecv,
    ysend,
    yrecv,
    got,
    home,
    ext,
    flux_z,
    picked,
    load_sem,
    plane_sem,
    final_sem,
    index_sem,
    store_sem,
    halo_send,
    halo_recv,
    pay_send,
    pay_recv,
    back_send,
    back_recv,
):
    n = n_gx * n_gy
    depth, height, width = rho_ref.shape
    cap = map_hbm.shape[1] // n
    gx = lax.axis_index("gx")
    gy = lax.axis_index("gy")
    me = gx * n_gy + gy

    def place(d):
        return (d // n_gy, lax.rem(d, n_gy))

    def ahead(k):
        x = lax.rem(gx + lax.rem(k, n_gx), n_gx)
        return x * n_gy + lax.rem(gy + k // n_gx, n_gy)

    def behind(k):
        x = lax.rem(gx + n_gx - lax.rem(k, n_gx), n_gx)
        return x * n_gy + lax.rem(gy + n_gy - k // n_gx, n_gy)

    barrier = pltpu.get_barrier_semaphore()

    def greet(k, carry):
        d = lax.rem(me + k, n)
        pl.semaphore_signal(barrier, inc=1, device_id=place(d), device_id_type=MESH)
        return carry

    loads = [
        pltpu.make_async_copy(src, dst, load_sem.at[i])
        for i, (src, dst) in enumerate(
            (
                (rank_hbm, rank_row),
                (map_hbm, map_ref),
                (rank_hbm, rank_ref),
                (count_hbm, count_ref),
                (ex_hbm, ex_ref),
                (mass_hbm, mass_ref),
                (motion_hbm, motion_ref),
                (kelvin_hbm, kelvin_ref),
                (vox_hbm, vox_ref),
                (lab_hbm, lab_ref),
                (rho_hbm, rho_ref),
                (vel_hbm, vel_ref),
                (temp_hbm, temp_ref),
            )
        )
    ]
    for load in loads:
        load.start()
    lax.fori_loop(1, n, greet, 0)
    for load in loads[:10]:
        load.wait()
    bin_grains(
        rank_ref,
        count_ref,
        ex_ref,
        mass_ref,
        motion_ref,
        kelvin_ref,
        vox_ref,
        lab_ref,
        dense,
        calm_ref,
        pull_ref,
    )
    place_pay(rank_row, dense, pay_ref, cap)

    def outward(k):
        d = ahead(k)
        return pltpu.make_async_remote_copy(
            src_ref=pay_ref.at[d],
            dst_ref=got.at[me],
            send_sem=pay_send.at[k],
            recv_sem=pay_recv.at[k],
            device_id=place(d),
            device_id_type=MESH,
        )

    def send_out(k, carry):
        outward(k).start()
        return carry

    pl.semaphore_wait(barrier, n - 1)
    early = 1 + n // 4
    lax.fori_loop(1, early, send_out, 0)
    stores = [
        pltpu.make_async_copy(src, dst, store_sem.at[i])
        for i, (src, dst) in enumerate(
            ((calm_ref, calm_out), (pull_ref, pull_out), (home, ret_out))
        )
    ]
    for store in stores[:2]:
        store.start()
    for load in loads[10:]:
        load.wait()

    def prim(f, z, rows):
        if f == 0:
            return rho_ref[z, rows, :]
        if f == 4:
            return temp_ref[z, rows, :]
        return vel_ref[f - 1, z, rows, :]

    whole = pl.ds(0, height)
    lanes = lax.broadcasted_iota(jnp.int32, (height, width), 1)

    def pack(z, carry):
        low, high = carry
        for f in range(5):
            spot = f * depth + z
            x = prim(f, z, whole)
            ysend[0, f, pl.ds(z, 1), :] = x[0:1]
            ysend[1, f, pl.ds(z, 1), :] = x[height - 1 : height]
            low = jnp.where(lanes == spot, pltpu.roll(x, spot, 1), low)
            high = jnp.where(lanes == spot, pltpu.roll(x, spot + 1, 1), high)
        return (low, high)

    zero = jnp.zeros((height, width), jnp.float32)
    low, high = lax.fori_loop(0, depth, pack, (zero, zero))
    xsend[0] = low
    xsend[1] = high

    def halo(which, side, device):
        src, dst = ((xsend, xrecv), (ysend, yrecv))[which]
        return pltpu.make_async_remote_copy(
            src_ref=src.at[side],
            dst_ref=dst.at[1 - side],
            send_sem=halo_send.at[2 * which + side],
            recv_sem=halo_recv.at[2 * which + 1 - side],
            device_id=device,
            device_id_type=MESH,
        )

    sides = (
        (0, 0, gx > 0, (gx - 1, gy)),
        (0, 1, gx < n_gx - 1, (gx + 1, gy)),
        (1, 0, gy > 0, (gx, gy - 1)),
        (1, 1, gy < n_gy - 1, (gx, gy + 1)),
    )
    for which, side, there, device in sides:

        @pl.when(there)
        def _(which=which, side=side, device=device):
            halo(which, side, device).start()

    lax.fori_loop(early, n, send_out, 0)

    blocks = depth * height
    number = lax.broadcasted_iota(jnp.int32, index_row.shape, 0) * width
    number = number + lax.broadcasted_iota(jnp.int32, index_row.shape, 1)

    def mark(s, index):
        for r in range(cap):
            i = s * cap + r
            index = jnp.where(number == map_ref[0, i], blocks + i, index)
        return index

    index_row[...] = lax.fori_loop(0, n, mark, number)
    index_copy = pltpu.make_async_copy(index_row, index_ref, index_sem)
    index_copy.start()

    for which, side, there, device in sides:
        recv = (xrecv, yrecv)[which]

        @pl.when(there)
        def _(which=which, side=side, device=device):
            pltpu.make_async_remote_copy(
                src_ref=(xsend, ysend)[which].at[side],
                dst_ref=(xrecv, yrecv)[which].at[side],
                send_sem=halo_send.at[2 * which + side],
                recv_sem=halo_recv.at[2 * which + side],
                device_id=device,
                device_id_type=MESH,
            ).wait()

        @pl.when(jnp.logical_not(there))
        def _(recv=recv, side=side):
            recv[side] = jnp.ones(recv.shape[1:], jnp.float32)

    west, east = gx == 0, gx == n_gx - 1
    south, north = gy == 0, gy == n_gy - 1
    flux_z[...] = jnp.zeros_like(flux_z)
    ext[...] = jnp.ones_like(ext)
    chunk = 32 if height % 32 == 0 else height
    tile = (chunk, width)
    lane = lax.broadcasted_iota(jnp.int32, tile, 1)
    row = lax.broadcasted_iota(jnp.int32, (chunk + 8, width), 0)
    first, last = lane == 0, lane == width - 1
    wall_low = jnp.logical_and(first, west)
    wall_high = jnp.logical_and(last, east)

    def plane_out(z):
        rows = pl.ds(z * height, height)
        return pltpu.make_async_copy(
            adv_ref.at[0, rows, :], adv_out.at[0, rows, :], plane_sem.at[z]
        )

    def final_out(z):
        rows = pl.ds(z * height, height)
        return pltpu.make_async_copy(
            fin_ref.at[:, rows, :], adv_out.at[pl.ds(1, back), rows, :], final_sem.at[z]
        )

    def plane(z, carry):
        above = jnp.minimum(z + 1, depth - 1)
        at_top = z == depth - 1
        here = conserve([prim(f, z, whole) for f in range(5)])
        for f in range(5):
            ext[f, 8 : 8 + height, :] = here[f]
        ext[5, 8 : 8 + height, :] = prim(2, z, whole)
        for side, at in ((0, 7), (1, 8 + height)):
            edge = [yrecv[side, f, pl.ds(z, 1), :] for f in range(5)]
            for f, q in enumerate(conserve(edge)):
                ext[f, at : at + 1, :] = q
            ext[5, at : at + 1, :] = edge[2]
        for y0 in range(0, height, chunk):
            rows = pl.ds(y0, chunk)
            own = [prim(f, z, rows) for f in range(5)]
            cons = conserve(own)
            change = [0.0] * 5
            up = [prim(f, above, rows) for f in range(5)]
            flux = face(cons, conserve(up), own[3], up[3], at_top)
            for f in range(5):
                change[f] = flux[f] - flux_z[f, rows, :]
                flux_z[f, rows, :] = flux[f]
            lower = [ext[f, pl.ds(7 + y0, chunk + 8), :] for f in range(6)]
            upper = [ext[f, pl.ds(8 + y0, chunk + 8), :] for f in range(6)]
            wall = False
            if y0 == 0:
                wall = jnp.logical_and(row == 0, south)
            if y0 + chunk == height:
                wall = jnp.logical_or(wall, jnp.logical_and(row == chunk, north))
            flux = face(lower[:5], upper[:5], lower[5], upper[5], wall)
            for f in range(5):
                change[f] = change[f] + (flux[f][1 : chunk + 1] - flux[f][:chunk])
            left, right = [], []
            for f in range(5):
                spot = f * depth + z
                left.append(
                    jnp.where(
                        first,
                        pltpu.roll(xrecv[0, rows, :], lax.rem(width - spot, width), 1),
                        pltpu.roll(own[f], 1, 1),
                    )
                )
                right.append(
                    jnp.where(
                        last,
                        pltpu.roll(xrecv[1, rows, :], width - 1 - spot, 1),
                        pltpu.roll(own[f], width - 1, 1),
                    )
                )
            flux = face(conserve(left), cons, left[1], own[1], wall_low)
            for f in range(5):
                change[f] = change[f] - flux[f]
            flux = face(cons, conserve(right), own[1], right[1], wall_high)
            for f in range(5):
                change[f] = change[f] + flux[f]
            fresh = [cons[f] - step_ratio * change[f] for f in range(5)]
            scale = 1.0 / fresh[0]
            out = pl.ds(z * height + y0, chunk)
            adv_ref[0, out, :] = fresh[0]
            for f in range(1, 5):
                adv_ref[f, out, :] = fresh[f] * scale
        plane_out(z).start()
        return carry

    lax.fori_loop(0, depth, plane, 0)

    def pick(s, carry):
        at = [jnp.maximum(map_ref[0, s * cap + r], 0) for r in range(cap)]
        for f in range(5):
            found = [adv_ref[f, pl.ds(b, 1), :] for b in at]
            picked[s, f * cap : (f + 1) * cap, :] = jnp.concatenate(found, 0)
        return carry

    lax.fori_loop(0, n, pick, 0)

    def part(ref, s, j):
        return ref[s, j * cap : (j + 1) * cap, :]

    def couple(ref, s):
        g = part(picked, s, 0)
        scale = 1.0 / (g + part(ref, s, 0))
        fresh = [(g * part(picked, s, 1 + c) + part(ref, s, 1 + c)) * scale for c in range(3)]
        fresh.append((g * part(picked, s, 4) + part(ref, s, 4)) / (g + part(ref, s, 5)))
        for j in range(back):
            new_ref[s, j * cap : (j + 1) * cap, :] = fresh[j]
            adv_ref[1 + j, pl.ds(blocks + s * cap, cap), :] = fresh[j]

    couple(pay_ref, me)
    home[me] = new_ref[me]

    def inward(k):
        d = behind(k)
        return pltpu.make_async_remote_copy(
            src_ref=new_ref.at[d],
            dst_ref=home.at[me],
            send_sem=back_send.at[k],
            recv_sem=back_recv.at[k],
            device_id=place(d),
            device_id_type=MESH,
        )

    def answer(k, carry):
        d = behind(k)
        outward(k).wait()
        couple(got, d)
        inward(k).start()
        return carry

    lax.fori_loop(1, n, answer, 0)

    index_copy.wait()
    unroll = 8

    def assemble(z, carry):
        def some(i, carry):
            b = z * height + i * unroll
            at = [index_ref[b // width, lax.rem(b, width) + u] for u in range(unroll)]
            for j in range(back):
                found = [adv_ref[1 + j, pl.ds(source, 1), :] for source in at]
                fin_ref[j, pl.ds(b, unroll), :] = jnp.concatenate(found, 0)
            return carry

        lax.fori_loop(0, height // unroll, some, 0)
        final_out(z).start()
        return carry

    lax.fori_loop(0, depth, assemble, 0)

    def finish(k, carry):
        inward(k).wait()
        return carry

    lax.fori_loop(1, n, finish, 0)
    stores[2].start()
    for store in stores:
        store.wait()
    for z in range(depth):
        plane_out(z).wait()
        final_out(z).wait()


def final_kernel(
    cap,
    rank_ref,
    adv_ref,
    ret_hbm,
    calm_hbm,
    pull_hbm,
    out_ref,
    solid_out,
    held,
    ret_ref,
    calm_ref,
    pull_ref,
    solid_ref,
    load_sem,
    store_sem,
):
    slots = rank_ref.shape[0]
    fields, blocks, width = adv_ref.shape
    loads = [
        pltpu.make_async_copy(src, dst, load_sem.at[i])
        for i, (src, dst) in enumerate(
            [(ret_hbm, ret_ref), (calm_hbm, calm_ref), (pull_hbm, pull_ref)]
            + [(adv_ref.at[f], held.at[f]) for f in range(fields)]
        )
    ]
    stores = [
        pltpu.make_async_copy(src, dst, store_sem.at[i])
        for i, (src, dst) in enumerate(
            [(held.at[f], out_ref.at[f]) for f in range(fields)] + [(solid_ref, solid_out)]
        )
    ]
    for load in loads:
        load.start()
    for load in loads[:3]:
        load.wait()
    for f in range(2):
        loads[3 + f].wait()
        stores[f].start()
    unroll = 8

    def solid(i, carry):
        for u in range(unroll):
            k = i * unroll + u
            v = jnp.maximum(rank_ref[k], 0)
            s = v // cap
            r = v % cap
            rows = [ret_ref[s, pl.ds(j * cap + r, 1), :] for j in range(back)]
            for j in range(back):
                solid_ref[j, pl.ds(2 * k, 2), :] = jnp.broadcast_to(rows[j], (2, width))
        return carry

    lax.fori_loop(0, slots // unroll, solid, 0)
    for j in range(back):
        solid_ref[j] = calm_ref[j] + pull_ref[j // 3] * solid_ref[j]
    for f in range(2, fields):
        loads[3 + f].wait()
        stores[f].start()
    stores[fields].start()
    for store in stores:
        store.wait()


def per_device(
    n_gx,
    n_gy,
    gaseous_rho,
    gaseous_flow_vector,
    gaseous_kelvin,
    sender_tile_map,
    receiver_arrival_rank,
    bin_active_number,
    grain_inertia,
    grain_motion_vector,
    grain_kelvin,
    grain_voxel_number,
    grain_substance_label,
    exchange_factor,
):
    n = n_gx * n_gy
    depth, height, width = gaseous_rho.shape
    slots, padding = grain_inertia.shape
    cap = sender_tile_map.shape[1] // n
    blocks = depth * height
    f32, i32 = jnp.float32, jnp.int32
    shape = jax.ShapeDtypeStruct
    dma = pltpu.SemaphoreType.DMA
    adv, ret, calm, pull = pl.pallas_call(
        functools.partial(grid_kernel, n_gx, n_gy),
        out_shape=(
            shape((5, blocks, width), f32),
            shape((n, back * cap, width), f32),
            shape((back, 2 * slots, width), f32),
            shape((2, 2 * slots, width), f32),
        ),
        in_specs=[ANY] * 12,
        out_specs=(ANY,) * 4,
        scratch_shapes=[
            pltpu.VMEM((5, blocks + n * cap, width), f32),
            pltpu.VMEM((back, blocks, width), f32),
            pltpu.VMEM((blocks // width, width), i32),
            pltpu.SMEM((blocks // width, width), i32),
            pltpu.VMEM((n, back * cap, width), f32),
            pltpu.VMEM((back, 2 * slots, width), f32),
            pltpu.VMEM((2, 2 * slots, width), f32),
            pltpu.VMEM((depth, height, width), f32),
            pltpu.VMEM((3, depth, height, width), f32),
            pltpu.VMEM((depth, height, width), f32),
            pltpu.VMEM((slots, padding), f32),
            pltpu.VMEM((3, slots, padding), f32),
            pltpu.VMEM((slots, padding), f32),
            pltpu.VMEM((slots, padding), i32),
            pltpu.VMEM((slots, padding), i32),
            pltpu.VMEM((1, slots), i32),
            pltpu.SMEM((1, n * cap), i32),
            pltpu.SMEM((1, slots), i32),
            pltpu.SMEM((1, slots), i32),
            pltpu.SMEM((2, 2), f32),
            pltpu.VMEM((sent, slots, width), f32),
            pltpu.VMEM((n, sent * cap, width), f32),
            pltpu.VMEM((2, height, width), f32),
            pltpu.VMEM((2, height, width), f32),
            pltpu.VMEM((2, 5, depth, width), f32),
            pltpu.VMEM((2, 5, depth, width), f32),
            pltpu.VMEM((n, sent * cap, width), f32),
            pltpu.VMEM((n, back * cap, width), f32),
            pltpu.VMEM((6, height + 16, width), f32),
            pltpu.VMEM((5, height, width), f32),
            pltpu.VMEM((n, 5 * cap, width), f32),
            dma((13,)),
            dma((depth,)),
            dma((depth,)),
            dma,
            dma((3,)),
            dma((4,)),
            dma((4,)),
            dma((n,)),
            dma((n,)),
            dma((n,)),
            dma((n,)),
        ],
        compiler_params=pltpu.CompilerParams(
            collective_id=0, has_side_effects=True, vmem_limit_bytes=limit
        ),
        name="advance_and_couple",
    )(
        gaseous_rho,
        gaseous_flow_vector,
        gaseous_kelvin,
        sender_tile_map,
        receiver_arrival_rank.reshape(1, slots),
        bin_active_number.reshape(1, slots),
        grain_inertia,
        grain_motion_vector,
        grain_kelvin,
        grain_voxel_number,
        grain_substance_label,
        exchange_factor,
    )
    final, solid = pl.pallas_call(
        functools.partial(final_kernel, cap),
        out_shape=(shape((5, blocks, width), f32), shape((back, 2 * slots, width), f32)),
        in_specs=[SMEM] + [ANY] * 4,
        out_specs=(ANY, ANY),
        scratch_shapes=[
            pltpu.VMEM((5, blocks, width), f32),
            pltpu.VMEM((n, back * cap, width), f32),
            pltpu.VMEM((back, 2 * slots, width), f32),
            pltpu.VMEM((2, 2 * slots, width), f32),
            pltpu.VMEM((back, 2 * slots, width), f32),
            dma((8,)),
            dma((6,)),
        ],
        compiler_params=pltpu.CompilerParams(vmem_limit_bytes=limit),
        name="place_results",
    )(receiver_arrival_rank, adv, ret, calm, pull)
    return (
        final.reshape(5, depth, height, width),
        solid.reshape(back, slots, 2, width),
    )


def solution(mesh):
    placed = (
        P(None, "gy", "gx"),
        P(None, None, "gy", "gx"),
        P(None, "gy", "gx"),
        P(("gx", "gy"), None),
        P(("gx", "gy")),
        P(("gx", "gy")),
        P(("gx", "gy"), None),
        P(None, ("gx", "gy"), None),
        P(("gx", "gy"), None),
        P(("gx", "gy"), None),
        P(("gx", "gy"), None),
        P(),
    )
    return jax.shard_map(
        functools.partial(per_device, mesh.shape["gx"], mesh.shape["gy"]),
        mesh=mesh,
        in_specs=placed,
        out_specs=(P(None, None, "gy", "gx"), P(None, ("gx", "gy"), None, None)),
        check_vma=False,
    )
```

```python
import functools

import jax
import jax.numpy as jnp
from jax import lax
from jax.experimental import pallas as pl
from jax.experimental.pallas import tpu as pltpu
from jax.sharding import PartitionSpec as P

MESH = pl.DeviceIdType.MESH
ANY = pl.BlockSpec(memory_space=pl.ANY)
SMEM = pl.BlockSpec(memory_space=pltpu.SMEM)
step_ratio = 0.08
limit = 56 * 1024 * 1024
sent = 6
back = 4


def coefficients(ex_ref, m):
    rows = lax.broadcasted_iota(jnp.int32, (8, 128), 0)
    return jnp.where(rows < 4, ex_ref[m, 0], ex_ref[m, 1])


def bin_grains(
    rank_ref, count_ref, ex_ref, mass_ref, vel_ref, temp_ref, vox_ref, lab_ref, dense, calm_ref, pull_ref
):
    slots, padding = mass_ref.shape
    width = dense.shape[2]
    rows = lax.broadcasted_iota(jnp.int32, (8, padding), 0)
    lane = lax.broadcasted_iota(jnp.int32, (1, padding), 1)
    cells = lax.broadcasted_iota(jnp.int32, (width, padding), 0)
    factor = [coefficients(ex_ref, m) for m in range(2)]
    unroll = 8

    def body(i, carry):
        for u in range(unroll):
            k = i * unroll + u
            here = pl.ds(k, 1)
            mass = jnp.where(lane < count_ref[0, k], mass_ref[here, :], 0.0)
            base = jnp.where(rows == 4, temp_ref[here, :], 1.0)
            for c in range(3):
                base = jnp.where(rows == c + 1, vel_ref[c, here, :], base)
            base = base * mass
            label = lab_ref[here, :]
            values = jnp.concatenate(
                [jnp.where(label == 0, base, 0.0), jnp.where(label == 1, base, 0.0)], 0
            )
            onehot = jnp.where(cells == vox_ref[here, :], 1.0, 0.0).astype(jnp.bfloat16)
            total = lax.dot_general(
                jnp.concatenate(split(values, 2), 0),
                onehot,
                (((1,), (1,)), ((), ())),
                preferred_element_type=jnp.float32,
            )
            total = total[:16] + total[16:]
            pay = 0.0
            live = jnp.where(rank_ref[0, k] >= 0, 1.0, 0.0)
            for m in range(2):
                part = total[8 * m : 8 * m + 8]
                scale = 1.0 / (part[0:1] + factor[m])
                pull = factor[m] * scale
                pay = pay + pull * part
                calm = part * scale * live
                pull = pull * live
                for j in range(back):
                    calm_ref[j, pl.ds(2 * k + m, 1), :] = calm[1 + j : 2 + j]
                for j in range(2):
                    pull_ref[j, pl.ds(2 * k + m, 1), :] = pull[1 + 3 * j : 2 + 3 * j]
            for j in range(sent):
                dense[j, here, :] = pay[j : j + 1]
        return carry

    lax.fori_loop(0, slots // unroll, body, 0)


def split(x, parts):
    out = []
    for _ in range(parts):
        out.append(x.astype(jnp.bfloat16))
        x = x - out[-1].astype(jnp.float32)
    return out


def place_pay(rank_row, dense, pay_ref, cap):
    n = pay_ref.shape[0]
    slots = dense.shape[1]
    position = lax.broadcasted_iota(jnp.int32, (n * cap, slots), 0)
    onehot = jnp.where(position == rank_row[...], 1.0, 0.0).astype(jnp.bfloat16)
    onehot = jnp.concatenate([onehot] * 3, 1)
    width = dense.shape[2]
    for j in range(0, sent, 2):
        pair = [jnp.concatenate(split(dense[j + i], 3), 0) for i in range(2)]
        total = jnp.dot(onehot, jnp.concatenate(pair, 1), preferred_element_type=jnp.float32)
        for s in range(n):
            for i in range(2):
                pay_ref[s, (j + i) * cap : (j + i + 1) * cap, :] = total[
                    s * cap : (s + 1) * cap, i * width : (i + 1) * width
                ]


def inverse(x):
    near = pl.reciprocal(x, approx=True)
    return near * (2.0 - x * near)


def face(a, b, ua, ub, wall):
    speed = 0.5 * (ua + ub) - (2.0 * step_ratio) * (b[4] - a[4]) * inverse(a[0] + b[0])
    speed = jnp.where(wall, 0.0, speed)
    ahead = speed > 0
    return [speed * jnp.where(ahead, x, y) for x, y in zip(a, b)]


def conserve(prim):
    rho = prim[0]
    return [rho] + [rho * q for q in prim[1:]]


def grid_kernel(
    n_gx,
    n_gy,
    rho_hbm,
    vel_hbm,
    temp_hbm,
    map_hbm,
    rank_hbm,
    count_hbm,
    mass_hbm,
    motion_hbm,
    kelvin_hbm,
    vox_hbm,
    lab_hbm,
    ex_hbm,
    adv_out,
    ret_out,
    calm_out,
    pull_out,
    adv_ref,
    fin_ref,
    index_row,
    index_ref,
    new_ref,
    calm_ref,
    pull_ref,
    rho_ref,
    vel_ref,
    temp_ref,
    mass_ref,
    motion_ref,
    kelvin_ref,
    vox_ref,
    lab_ref,
    rank_row,
    map_ref,
    rank_ref,
    count_ref,
    ex_ref,
    dense,
    pay_ref,
    xsend,
    xrecv,
    ysend,
    yrecv,
    got,
    home,
    ext,
    flux_z,
    edge_x,
    picked,
    load_sem,
    plane_sem,
    final_sem,
    index_sem,
    store_sem,
    halo_send,
    halo_recv,
    pay_send,
    pay_recv,
    back_send,
    back_recv,
):
    n = n_gx * n_gy
    depth, height, width = rho_ref.shape
    cap = map_hbm.shape[1] // n
    gx = lax.axis_index("gx")
    gy = lax.axis_index("gy")
    me = gx * n_gy + gy

    def place(d):
        return (d // n_gy, lax.rem(d, n_gy))

    def ahead(k):
        x = lax.rem(gx + lax.rem(k, n_gx), n_gx)
        return x * n_gy + lax.rem(gy + k // n_gx, n_gy)

    def behind(k):
        x = lax.rem(gx + n_gx - lax.rem(k, n_gx), n_gx)
        return x * n_gy + lax.rem(gy + n_gy - k // n_gx, n_gy)

    barrier = pltpu.get_barrier_semaphore()

    def greet(k, carry):
        d = lax.rem(me + k, n)
        pl.semaphore_signal(barrier, inc=1, device_id=place(d), device_id_type=MESH)
        return carry

    loads = [
        pltpu.make_async_copy(src, dst, load_sem.at[i])
        for i, (src, dst) in enumerate(
            (
                (rank_hbm, rank_row),
                (map_hbm, map_ref),
                (rank_hbm, rank_ref),
                (count_hbm, count_ref),
                (ex_hbm, ex_ref),
                (mass_hbm, mass_ref),
                (motion_hbm, motion_ref),
                (kelvin_hbm, kelvin_ref),
                (vox_hbm, vox_ref),
                (lab_hbm, lab_ref),
                (rho_hbm, rho_ref),
                (vel_hbm, vel_ref),
                (temp_hbm, temp_ref),
            )
        )
    ]
    for load in loads:
        load.start()
    lax.fori_loop(1, n, greet, 0)
    for load in loads[:10]:
        load.wait()
    bin_grains(
        rank_ref,
        count_ref,
        ex_ref,
        mass_ref,
        motion_ref,
        kelvin_ref,
        vox_ref,
        lab_ref,
        dense,
        calm_ref,
        pull_ref,
    )
    place_pay(rank_row, dense, pay_ref, cap)

    def outward(k):
        d = ahead(k)
        return pltpu.make_async_remote_copy(
            src_ref=pay_ref.at[d],
            dst_ref=got.at[me],
            send_sem=pay_send.at[k],
            recv_sem=pay_recv.at[k],
            device_id=place(d),
            device_id_type=MESH,
        )

    def send_out(k, carry):
        outward(k).start()
        return carry

    pl.semaphore_wait(barrier, n - 1)
    early = 1 + n // 4
    lax.fori_loop(1, early, send_out, 0)
    stores = [
        pltpu.make_async_copy(src, dst, store_sem.at[i])
        for i, (src, dst) in enumerate(
            ((calm_ref, calm_out), (pull_ref, pull_out), (home, ret_out))
        )
    ]
    for store in stores[:2]:
        store.start()
    for load in loads[10:]:
        load.wait()

    def prim(f, z, rows):
        if f == 0:
            return rho_ref[z, rows, :]
        if f == 4:
            return temp_ref[z, rows, :]
        return vel_ref[f - 1, z, rows, :]

    whole = pl.ds(0, height)
    lanes = lax.broadcasted_iota(jnp.int32, (height, width), 1)

    def pack(z, carry):
        low, high = carry
        for f in range(5):
            spot = f * depth + z
            x = prim(f, z, whole)
            ysend[0, f, pl.ds(z, 1), :] = x[0:1]
            ysend[1, f, pl.ds(z, 1), :] = x[height - 1 : height]
            low = jnp.where(lanes == spot, pltpu.roll(x, spot, 1), low)
            high = jnp.where(lanes == spot, pltpu.roll(x, spot + 1, 1), high)
        return (low, high)

    zero = jnp.zeros((height, width), jnp.float32)
    low, high = lax.fori_loop(0, depth, pack, (zero, zero))
    xsend[0] = low
    xsend[1] = high

    def halo(which, side, device):
        src, dst = ((xsend, xrecv), (ysend, yrecv))[which]
        return pltpu.make_async_remote_copy(
            src_ref=src.at[side],
            dst_ref=dst.at[1 - side],
            send_sem=halo_send.at[2 * which + side],
            recv_sem=halo_recv.at[2 * which + 1 - side],
            device_id=device,
            device_id_type=MESH,
        )

    sides = (
        (0, 0, gx > 0, (gx - 1, gy)),
        (0, 1, gx < n_gx - 1, (gx + 1, gy)),
        (1, 0, gy > 0, (gx, gy - 1)),
        (1, 1, gy < n_gy - 1, (gx, gy + 1)),
    )
    for which, side, there, device in sides:

        @pl.when(there)
        def _(which=which, side=side, device=device):
            halo(which, side, device).start()

    lax.fori_loop(early, n, send_out, 0)

    blocks = depth * height
    for which, side, there, device in sides:
        recv = (xrecv, yrecv)[which]

        @pl.when(there)
        def _(which=which, side=side, device=device):
            pltpu.make_async_remote_copy(
                src_ref=(xsend, ysend)[which].at[side],
                dst_ref=(xrecv, yrecv)[which].at[side],
                send_sem=halo_send.at[2 * which + side],
                recv_sem=halo_recv.at[2 * which + side],
                device_id=device,
                device_id_type=MESH,
            ).wait()

        @pl.when(jnp.logical_not(there))
        def _(recv=recv, side=side):
            recv[side] = jnp.ones(recv.shape[1:], jnp.float32)

    west, east = gx == 0, gx == n_gx - 1
    south, north = gy == 0, gy == n_gy - 1
    flux_z[...] = jnp.zeros_like(flux_z)
    ext[...] = jnp.ones_like(ext)
    chunk = 32 if height % 32 == 0 else height
    tile = (chunk, width)
    lane = lax.broadcasted_iota(jnp.int32, tile, 1)
    row = lax.broadcasted_iota(jnp.int32, (chunk + 8, width), 0)
    first, last = lane == 0, lane == width - 1
    wall_low = jnp.logical_and(first, west)

    def lined(ref):
        packed = ref[1]
        return [packed] + [pltpu.roll(packed, width - f * depth, 1) for f in range(1, 5)]

    inner, beyond = lined(xsend), lined(xrecv)
    rim = face(conserve(inner), conserve(beyond), inner[1], beyond[1], east)
    for f in range(5):
        edge_x[f] = rim[f]

    def plane_out(z):
        rows = pl.ds(z * height, height)
        return pltpu.make_async_copy(
            adv_ref.at[0, rows, :], adv_out.at[0, rows, :], plane_sem.at[z]
        )

    def final_out(z):
        rows = pl.ds(z * height, height)
        return pltpu.make_async_copy(
            fin_ref.at[:, rows, :], adv_out.at[pl.ds(1, back), rows, :], final_sem.at[z]
        )

    def plane(z, carry):
        above = jnp.minimum(z + 1, depth - 1)
        at_top = z == depth - 1
        here = conserve([prim(f, z, whole) for f in range(5)])
        for f in range(5):
            ext[f, 8 : 8 + height, :] = here[f]
        ext[5, 8 : 8 + height, :] = prim(2, z, whole)
        for side, at in ((0, 7), (1, 8 + height)):
            edge = [yrecv[side, f, pl.ds(z, 1), :] for f in range(5)]
            for f, q in enumerate(conserve(edge)):
                ext[f, at : at + 1, :] = q
            ext[5, at : at + 1, :] = edge[2]
        for y0 in range(0, height, chunk):
            rows = pl.ds(y0, chunk)
            own = [prim(f, z, rows) for f in range(5)]
            cons = conserve(own)
            change = [0.0] * 5
            up = [prim(f, above, rows) for f in range(5)]
            flux = face(cons, conserve(up), own[3], up[3], at_top)
            for f in range(5):
                change[f] = flux[f] - flux_z[f, rows, :]
                flux_z[f, rows, :] = flux[f]
            lower = [ext[f, pl.ds(7 + y0, chunk + 8), :] for f in range(6)]
            upper = [ext[f, pl.ds(8 + y0, chunk + 8), :] for f in range(6)]
            wall = False
            if y0 == 0:
                wall = jnp.logical_and(row == 0, south)
            if y0 + chunk == height:
                wall = jnp.logical_or(wall, jnp.logical_and(row == chunk, north))
            flux = face(lower[:5], upper[:5], lower[5], upper[5], wall)
            for f in range(5):
                change[f] = change[f] + (flux[f][1 : chunk + 1] - flux[f][:chunk])
            left = []
            for f in range(5):
                spot = f * depth + z
                left.append(
                    jnp.where(
                        first,
                        pltpu.roll(xrecv[0, rows, :], lax.rem(width - spot, width), 1),
                        pltpu.roll(own[f], 1, 1),
                    )
                )
            flux = face(conserve(left), cons, left[1], own[1], wall_low)
            for f in range(5):
                over = jnp.where(
                    last,
                    pltpu.roll(edge_x[f, rows, :], width - 1 - z, 1),
                    pltpu.roll(flux[f], width - 1, 1),
                )
                change[f] = change[f] + (over - flux[f])
            fresh = [cons[f] - step_ratio * change[f] for f in range(5)]
            scale = inverse(fresh[0])
            out = pl.ds(z * height + y0, chunk)
            adv_ref[0, out, :] = fresh[0]
            for f in range(1, 5):
                adv_ref[f, out, :] = fresh[f] * scale
        plane_out(z).start()
        return carry

    lax.fori_loop(0, depth, plane, 0)

    def pick(s, carry):
        at = [jnp.maximum(map_ref[0, s * cap + r], 0) for r in range(cap)]
        for f in range(5):
            found = [adv_ref[f, pl.ds(b, 1), :] for b in at]
            picked[s, f * cap : (f + 1) * cap, :] = jnp.concatenate(found, 0)
        return carry

    lax.fori_loop(0, n, pick, 0)

    def part(ref, s, j):
        return ref[s, j * cap : (j + 1) * cap, :]

    def couple(ref, s):
        g = part(picked, s, 0)
        scale = 1.0 / (g + part(ref, s, 0))
        fresh = [(g * part(picked, s, 1 + c) + part(ref, s, 1 + c)) * scale for c in range(3)]
        fresh.append((g * part(picked, s, 4) + part(ref, s, 4)) / (g + part(ref, s, 5)))
        for j in range(back):
            new_ref[s, j * cap : (j + 1) * cap, :] = fresh[j]
            adv_ref[1 + j, pl.ds(blocks + s * cap, cap), :] = fresh[j]

    couple(pay_ref, me)
    home[me] = new_ref[me]

    def inward(k):
        d = behind(k)
        return pltpu.make_async_remote_copy(
            src_ref=new_ref.at[d],
            dst_ref=home.at[me],
            send_sem=back_send.at[k],
            recv_sem=back_recv.at[k],
            device_id=place(d),
            device_id_type=MESH,
        )

    def answer(k, carry):
        d = behind(k)
        outward(k).wait()
        couple(got, d)
        inward(k).start()
        return carry

    lax.fori_loop(1, n, answer, 0)

    number = lax.broadcasted_iota(jnp.int32, index_row.shape, 0) * width
    number = number + lax.broadcasted_iota(jnp.int32, index_row.shape, 1)

    def mark(s, index):
        for r in range(cap):
            i = s * cap + r
            index = jnp.where(number == map_ref[0, i], blocks + i, index)
        return index

    index_row[...] = lax.fori_loop(0, n, mark, number)
    index_copy = pltpu.make_async_copy(index_row, index_ref, index_sem)
    index_copy.start()

    index_copy.wait()
    unroll = 8

    def assemble(z, carry):
        def some(i, carry):
            b = z * height + i * unroll
            at = [index_ref[b // width, lax.rem(b, width) + u] for u in range(unroll)]
            for j in range(back):
                found = [adv_ref[1 + j, pl.ds(source, 1), :] for source in at]
                fin_ref[j, pl.ds(b, unroll), :] = jnp.concatenate(found, 0)
            return carry

        lax.fori_loop(0, height // unroll, some, 0)
        final_out(z).start()
        return carry

    lax.fori_loop(0, depth, assemble, 0)

    def finish(k, carry):
        inward(k).wait()
        return carry

    lax.fori_loop(1, n, finish, 0)
    stores[2].start()
    for store in stores:
        store.wait()
    for z in range(depth):
        plane_out(z).wait()
        final_out(z).wait()


def final_kernel(
    cap,
    rank_ref,
    adv_ref,
    ret_hbm,
    calm_hbm,
    pull_hbm,
    out_ref,
    solid_out,
    held,
    ret_ref,
    calm_ref,
    pull_ref,
    solid_ref,
    load_sem,
    store_sem,
):
    slots = rank_ref.shape[0]
    fields, blocks, width = adv_ref.shape
    loads = [
        pltpu.make_async_copy(src, dst, load_sem.at[i])
        for i, (src, dst) in enumerate(
            [(ret_hbm, ret_ref), (calm_hbm, calm_ref), (pull_hbm, pull_ref)]
            + [(adv_ref.at[f], held.at[f]) for f in range(fields)]
        )
    ]
    stores = [
        pltpu.make_async_copy(src, dst, store_sem.at[i])
        for i, (src, dst) in enumerate(
            [(held.at[f], out_ref.at[f]) for f in range(fields)] + [(solid_ref, solid_out)]
        )
    ]
    for load in loads:
        load.start()
    for load in loads[:3]:
        load.wait()
    for f in range(2):
        loads[3 + f].wait()
        stores[f].start()
    unroll = 8

    def solid(i, carry):
        for u in range(unroll):
            k = i * unroll + u
            v = jnp.maximum(rank_ref[k], 0)
            s = v // cap
            r = v % cap
            rows = [ret_ref[s, pl.ds(j * cap + r, 1), :] for j in range(back)]
            for j in range(back):
                solid_ref[j, pl.ds(2 * k, 2), :] = jnp.broadcast_to(rows[j], (2, width))
        return carry

    lax.fori_loop(0, slots // unroll, solid, 0)
    for j in range(back):
        solid_ref[j] = calm_ref[j] + pull_ref[j // 3] * solid_ref[j]
    for f in range(2, fields):
        loads[3 + f].wait()
        stores[f].start()
    stores[fields].start()
    for store in stores:
        store.wait()


def per_device(
    n_gx,
    n_gy,
    gaseous_rho,
    gaseous_flow_vector,
    gaseous_kelvin,
    sender_tile_map,
    receiver_arrival_rank,
    bin_active_number,
    grain_inertia,
    grain_motion_vector,
    grain_kelvin,
    grain_voxel_number,
    grain_substance_label,
    exchange_factor,
):
    n = n_gx * n_gy
    depth, height, width = gaseous_rho.shape
    slots, padding = grain_inertia.shape
    cap = sender_tile_map.shape[1] // n
    blocks = depth * height
    f32, i32 = jnp.float32, jnp.int32
    shape = jax.ShapeDtypeStruct
    dma = pltpu.SemaphoreType.DMA
    adv, ret, calm, pull = pl.pallas_call(
        functools.partial(grid_kernel, n_gx, n_gy),
        out_shape=(
            shape((5, blocks, width), f32),
            shape((n, back * cap, width), f32),
            shape((back, 2 * slots, width), f32),
            shape((2, 2 * slots, width), f32),
        ),
        in_specs=[ANY] * 12,
        out_specs=(ANY,) * 4,
        scratch_shapes=[
            pltpu.VMEM((5, blocks + n * cap, width), f32),
            pltpu.VMEM((back, blocks, width), f32),
            pltpu.VMEM((blocks // width, width), i32),
            pltpu.SMEM((blocks // width, width), i32),
            pltpu.VMEM((n, back * cap, width), f32),
            pltpu.VMEM((back, 2 * slots, width), f32),
            pltpu.VMEM((2, 2 * slots, width), f32),
            pltpu.VMEM((depth, height, width), f32),
            pltpu.VMEM((3, depth, height, width), f32),
            pltpu.VMEM((depth, height, width), f32),
            pltpu.VMEM((slots, padding), f32),
            pltpu.VMEM((3, slots, padding), f32),
            pltpu.VMEM((slots, padding), f32),
            pltpu.VMEM((slots, padding), i32),
            pltpu.VMEM((slots, padding), i32),
            pltpu.VMEM((1, slots), i32),
            pltpu.SMEM((1, n * cap), i32),
            pltpu.SMEM((1, slots), i32),
            pltpu.SMEM((1, slots), i32),
            pltpu.SMEM((2, 2), f32),
            pltpu.VMEM((sent, slots, width), f32),
            pltpu.VMEM((n, sent * cap, width), f32),
            pltpu.VMEM((2, height, width), f32),
            pltpu.VMEM((2, height, width), f32),
            pltpu.VMEM((2, 5, depth, width), f32),
            pltpu.VMEM((2, 5, depth, width), f32),
            pltpu.VMEM((n, sent * cap, width), f32),
            pltpu.VMEM((n, back * cap, width), f32),
            pltpu.VMEM((6, height + 16, width), f32),
            pltpu.VMEM((5, height, width), f32),
            pltpu.VMEM((5, height, width), f32),
            pltpu.VMEM((n, 5 * cap, width), f32),
            dma((13,)),
            dma((depth,)),
            dma((depth,)),
            dma,
            dma((3,)),
            dma((4,)),
            dma((4,)),
            dma((n,)),
            dma((n,)),
            dma((n,)),
            dma((n,)),
        ],
        compiler_params=pltpu.CompilerParams(
            collective_id=0, has_side_effects=True, vmem_limit_bytes=limit
        ),
        name="advance_and_couple",
    )(
        gaseous_rho,
        gaseous_flow_vector,
        gaseous_kelvin,
        sender_tile_map,
        receiver_arrival_rank.reshape(1, slots),
        bin_active_number.reshape(1, slots),
        grain_inertia,
        grain_motion_vector,
        grain_kelvin,
        grain_voxel_number,
        grain_substance_label,
        exchange_factor,
    )
    final, solid = pl.pallas_call(
        functools.partial(final_kernel, cap),
        out_shape=(shape((5, blocks, width), f32), shape((back, 2 * slots, width), f32)),
        in_specs=[SMEM] + [ANY] * 4,
        out_specs=(ANY, ANY),
        scratch_shapes=[
            pltpu.VMEM((5, blocks, width), f32),
            pltpu.VMEM((n, back * cap, width), f32),
            pltpu.VMEM((back, 2 * slots, width), f32),
            pltpu.VMEM((2, 2 * slots, width), f32),
            pltpu.VMEM((back, 2 * slots, width), f32),
            dma((8,)),
            dma((6,)),
        ],
        compiler_params=pltpu.CompilerParams(vmem_limit_bytes=limit),
        name="place_results",
    )(receiver_arrival_rank, adv, ret, calm, pull)
    return (
        final.reshape(5, depth, height, width),
        solid.reshape(back, slots, 2, width),
    )


def solution(mesh):
    placed = (
        P(None, "gy", "gx"),
        P(None, None, "gy", "gx"),
        P(None, "gy", "gx"),
        P(("gx", "gy"), None),
        P(("gx", "gy")),
        P(("gx", "gy")),
        P(("gx", "gy"), None),
        P(None, ("gx", "gy"), None),
        P(("gx", "gy"), None),
        P(("gx", "gy"), None),
        P(("gx", "gy"), None),
        P(),
    )
    return jax.shard_map(
        functools.partial(per_device, mesh.shape["gx"], mesh.shape["gy"]),
        mesh=mesh,
        in_specs=placed,
        out_specs=(P(None, None, "gy", "gx"), P(None, ("gx", "gy"), None, None)),
        check_vma=False,
    )
```

```python
import functools

import jax
import jax.numpy as jnp
from jax import lax
from jax.experimental import pallas as pl
from jax.experimental.pallas import tpu as pltpu
from jax.sharding import PartitionSpec as P

MESH = pl.DeviceIdType.MESH
ANY = pl.BlockSpec(memory_space=pl.ANY)
SMEM = pl.BlockSpec(memory_space=pltpu.SMEM)
step_ratio = 0.08
limit = 56 * 1024 * 1024
sent = 6
back = 4


def coefficients(ex_ref, m):
    rows = lax.broadcasted_iota(jnp.int32, (8, 128), 0)
    return jnp.where(rows < 4, ex_ref[m, 0], ex_ref[m, 1])


def bin_grains(
    rank_ref, count_ref, ex_ref, mass_ref, vel_ref, temp_ref, vox_ref, lab_ref, dense, calm_ref, pull_ref
):
    slots, padding = mass_ref.shape
    width = dense.shape[2]
    rows = lax.broadcasted_iota(jnp.int32, (8, padding), 0)
    lane = lax.broadcasted_iota(jnp.int32, (1, padding), 1)
    cells = lax.broadcasted_iota(jnp.int32, (width, padding), 0)
    factor = [coefficients(ex_ref, m) for m in range(2)]
    unroll = 8

    def body(i, carry):
        for u in range(unroll):
            k = i * unroll + u
            here = pl.ds(k, 1)
            mass = jnp.where(lane < count_ref[0, k], mass_ref[here, :], 0.0)
            base = jnp.where(rows == 4, temp_ref[here, :], 1.0)
            for c in range(3):
                base = jnp.where(rows == c + 1, vel_ref[c, here, :], base)
            base = base * mass
            label = lab_ref[here, :]
            values = jnp.concatenate(
                [jnp.where(label == 0, base, 0.0), jnp.where(label == 1, base, 0.0)], 0
            )
            onehot = jnp.where(cells == vox_ref[here, :], 1.0, 0.0).astype(jnp.bfloat16)
            total = lax.dot_general(
                onehot,
                jnp.concatenate(split(values, 2), 0),
                (((1,), (1,)), ((), ())),
                preferred_element_type=jnp.float32,
            ).T
            total = total[:16] + total[16:]
            pay = 0.0
            live = jnp.where(rank_ref[0, k] >= 0, 1.0, 0.0)
            for m in range(2):
                part = total[8 * m : 8 * m + 8]
                scale = 1.0 / (part[0:1] + factor[m])
                pull = factor[m] * scale
                pay = pay + pull * part
                calm = part * scale * live
                pull = pull * live
                for j in range(back):
                    calm_ref[j, pl.ds(2 * k + m, 1), :] = calm[1 + j : 2 + j]
                for j in range(2):
                    pull_ref[j, pl.ds(2 * k + m, 1), :] = pull[1 + 3 * j : 2 + 3 * j]
            for j in range(sent):
                dense[j, here, :] = pay[j : j + 1]
        return carry

    lax.fori_loop(0, slots // unroll, body, 0)


def split(x, parts):
    out = []
    for _ in range(parts):
        out.append(x.astype(jnp.bfloat16))
        x = x - out[-1].astype(jnp.float32)
    return out


def place_pay(rank_row, dense, pay_ref, cap):
    n = pay_ref.shape[0]
    slots = dense.shape[1]
    position = lax.broadcasted_iota(jnp.int32, (n * cap, slots), 0)
    onehot = jnp.where(position == rank_row[...], 1.0, 0.0).astype(jnp.bfloat16)
    onehot = jnp.concatenate([onehot] * 3, 1)
    width = dense.shape[2]
    for j in range(0, sent, 2):
        pair = [jnp.concatenate(split(dense[j + i], 3), 0) for i in range(2)]
        total = jnp.dot(onehot, jnp.concatenate(pair, 1), preferred_element_type=jnp.float32)
        for s in range(n):
            for i in range(2):
                pay_ref[s, (j + i) * cap : (j + i + 1) * cap, :] = total[
                    s * cap : (s + 1) * cap, i * width : (i + 1) * width
                ]


def inverse(x):
    near = pl.reciprocal(x, approx=True)
    return near * (2.0 - x * near)


def face(a, b, ua, ub, wall):
    speed = 0.5 * (ua + ub) - (2.0 * step_ratio) * (b[4] - a[4]) * inverse(a[0] + b[0])
    speed = jnp.where(wall, 0.0, speed)
    ahead = speed > 0
    return [speed * jnp.where(ahead, x, y) for x, y in zip(a, b)]


def conserve(prim):
    rho = prim[0]
    return [rho] + [rho * q for q in prim[1:]]


def grid_kernel(
    n_gx,
    n_gy,
    rho_hbm,
    vel_hbm,
    temp_hbm,
    map_hbm,
    rank_hbm,
    count_hbm,
    mass_hbm,
    motion_hbm,
    kelvin_hbm,
    vox_hbm,
    lab_hbm,
    ex_hbm,
    adv_out,
    ret_out,
    calm_out,
    pull_out,
    adv_ref,
    fin_ref,
    index_row,
    index_ref,
    new_ref,
    calm_ref,
    pull_ref,
    rho_ref,
    vel_ref,
    temp_ref,
    mass_ref,
    motion_ref,
    kelvin_ref,
    vox_ref,
    lab_ref,
    rank_row,
    map_ref,
    rank_ref,
    count_ref,
    ex_ref,
    dense,
    pay_ref,
    xsend,
    xrecv,
    ysend,
    yrecv,
    got,
    home,
    ext,
    flux_z,
    edge_x,
    picked,
    load_sem,
    plane_sem,
    final_sem,
    index_sem,
    store_sem,
    halo_send,
    halo_recv,
    pay_send,
    pay_recv,
    back_send,
    back_recv,
):
    n = n_gx * n_gy
    depth, height, width = rho_ref.shape
    cap = map_hbm.shape[1] // n
    gx = lax.axis_index("gx")
    gy = lax.axis_index("gy")
    me = gx * n_gy + gy

    def place(d):
        return (d // n_gy, lax.rem(d, n_gy))

    def ahead(k):
        x = lax.rem(gx + lax.rem(k, n_gx), n_gx)
        return x * n_gy + lax.rem(gy + k // n_gx, n_gy)

    def behind(k):
        x = lax.rem(gx + n_gx - lax.rem(k, n_gx), n_gx)
        return x * n_gy + lax.rem(gy + n_gy - k // n_gx, n_gy)

    barrier = pltpu.get_barrier_semaphore()

    def greet(k, carry):
        d = lax.rem(me + k, n)
        pl.semaphore_signal(barrier, inc=1, device_id=place(d), device_id_type=MESH)
        return carry

    loads = [
        pltpu.make_async_copy(src, dst, load_sem.at[i])
        for i, (src, dst) in enumerate(
            (
                (rank_hbm, rank_row),
                (map_hbm, map_ref),
                (rank_hbm, rank_ref),
                (count_hbm, count_ref),
                (ex_hbm, ex_ref),
                (mass_hbm, mass_ref),
                (motion_hbm, motion_ref),
                (kelvin_hbm, kelvin_ref),
                (vox_hbm, vox_ref),
                (lab_hbm, lab_ref),
                (rho_hbm, rho_ref),
                (vel_hbm, vel_ref),
                (temp_hbm, temp_ref),
            )
        )
    ]
    for load in loads:
        load.start()
    lax.fori_loop(1, n, greet, 0)
    for load in loads[:10]:
        load.wait()
    bin_grains(
        rank_ref,
        count_ref,
        ex_ref,
        mass_ref,
        motion_ref,
        kelvin_ref,
        vox_ref,
        lab_ref,
        dense,
        calm_ref,
        pull_ref,
    )
    place_pay(rank_row, dense, pay_ref, cap)

    def outward(k):
        d = ahead(k)
        return pltpu.make_async_remote_copy(
            src_ref=pay_ref.at[d],
            dst_ref=got.at[me],
            send_sem=pay_send.at[k],
            recv_sem=pay_recv.at[k],
            device_id=place(d),
            device_id_type=MESH,
        )

    def send_out(k, carry):
        outward(k).start()
        return carry

    pl.semaphore_wait(barrier, n - 1)
    early = 1 + n // 4
    lax.fori_loop(1, early, send_out, 0)
    stores = [
        pltpu.make_async_copy(src, dst, store_sem.at[i])
        for i, (src, dst) in enumerate(
            ((calm_ref, calm_out), (pull_ref, pull_out), (home, ret_out))
        )
    ]
    for store in stores[:2]:
        store.start()
    for load in loads[10:]:
        load.wait()

    def prim(f, z, rows):
        if f == 0:
            return rho_ref[z, rows, :]
        if f == 4:
            return temp_ref[z, rows, :]
        return vel_ref[f - 1, z, rows, :]

    whole = pl.ds(0, height)
    lanes = lax.broadcasted_iota(jnp.int32, (height, width), 1)

    def pack(z, carry):
        low, high = carry
        for f in range(5):
            spot = f * depth + z
            x = prim(f, z, whole)
            ysend[0, f, pl.ds(z, 1), :] = x[0:1]
            ysend[1, f, pl.ds(z, 1), :] = x[height - 1 : height]
            low = jnp.where(lanes == spot, pltpu.roll(x, spot, 1), low)
            high = jnp.where(lanes == spot, pltpu.roll(x, spot + 1, 1), high)
        return (low, high)

    zero = jnp.zeros((height, width), jnp.float32)
    low, high = lax.fori_loop(0, depth, pack, (zero, zero))
    xsend[0] = low
    xsend[1] = high

    def halo(which, side, device):
        src, dst = ((xsend, xrecv), (ysend, yrecv))[which]
        return pltpu.make_async_remote_copy(
            src_ref=src.at[side],
            dst_ref=dst.at[1 - side],
            send_sem=halo_send.at[2 * which + side],
            recv_sem=halo_recv.at[2 * which + 1 - side],
            device_id=device,
            device_id_type=MESH,
        )

    sides = (
        (0, 0, gx > 0, (gx - 1, gy)),
        (0, 1, gx < n_gx - 1, (gx + 1, gy)),
        (1, 0, gy > 0, (gx, gy - 1)),
        (1, 1, gy < n_gy - 1, (gx, gy + 1)),
    )
    for which, side, there, device in sides:

        @pl.when(there)
        def _(which=which, side=side, device=device):
            halo(which, side, device).start()

    lax.fori_loop(early, n, send_out, 0)

    blocks = depth * height
    for which, side, there, device in sides:
        recv = (xrecv, yrecv)[which]

        @pl.when(there)
        def _(which=which, side=side, device=device):
            pltpu.make_async_remote_copy(
                src_ref=(xsend, ysend)[which].at[side],
                dst_ref=(xrecv, yrecv)[which].at[side],
                send_sem=halo_send.at[2 * which + side],
                recv_sem=halo_recv.at[2 * which + side],
                device_id=device,
                device_id_type=MESH,
            ).wait()

        @pl.when(jnp.logical_not(there))
        def _(recv=recv, side=side):
            recv[side] = jnp.ones(recv.shape[1:], jnp.float32)

    west, east = gx == 0, gx == n_gx - 1
    south, north = gy == 0, gy == n_gy - 1
    flux_z[...] = jnp.zeros_like(flux_z)
    ext[...] = jnp.ones_like(ext)
    chunk = 32 if height % 32 == 0 else height
    tile = (chunk, width)
    lane = lax.broadcasted_iota(jnp.int32, tile, 1)
    row = lax.broadcasted_iota(jnp.int32, (chunk + 8, width), 0)
    first, last = lane == 0, lane == width - 1
    wall_low = jnp.logical_and(first, west)

    def lined(ref):
        packed = ref[1]
        return [packed] + [pltpu.roll(packed, width - f * depth, 1) for f in range(1, 5)]

    inner, beyond = lined(xsend), lined(xrecv)
    rim = face(conserve(inner), conserve(beyond), inner[1], beyond[1], east)
    for f in range(5):
        edge_x[f] = rim[f]

    def plane_out(z):
        rows = pl.ds(z * height, height)
        return pltpu.make_async_copy(
            adv_ref.at[0, rows, :], adv_out.at[0, rows, :], plane_sem.at[z]
        )

    def final_out(z):
        rows = pl.ds(z * height, height)
        return pltpu.make_async_copy(
            fin_ref.at[:, rows, :], adv_out.at[pl.ds(1, back), rows, :], final_sem.at[z]
        )

    def plane(z, carry):
        above = jnp.minimum(z + 1, depth - 1)
        at_top = z == depth - 1
        here = conserve([prim(f, z, whole) for f in range(5)])
        for f in range(5):
            ext[f, 8 : 8 + height, :] = here[f]
        ext[5, 8 : 8 + height, :] = prim(2, z, whole)
        for side, at in ((0, 7), (1, 8 + height)):
            edge = [yrecv[side, f, pl.ds(z, 1), :] for f in range(5)]
            for f, q in enumerate(conserve(edge)):
                ext[f, at : at + 1, :] = q
            ext[5, at : at + 1, :] = edge[2]
        for y0 in range(0, height, chunk):
            rows = pl.ds(y0, chunk)
            own = [prim(f, z, rows) for f in range(5)]
            cons = conserve(own)
            change = [0.0] * 5
            up = [prim(f, above, rows) for f in range(5)]
            flux = face(cons, conserve(up), own[3], up[3], at_top)
            for f in range(5):
                change[f] = flux[f] - flux_z[f, rows, :]
                flux_z[f, rows, :] = flux[f]
            lower = [ext[f, pl.ds(7 + y0, chunk + 8), :] for f in range(6)]
            upper = [ext[f, pl.ds(8 + y0, chunk + 8), :] for f in range(6)]
            wall = False
            if y0 == 0:
                wall = jnp.logical_and(row == 0, south)
            if y0 + chunk == height:
                wall = jnp.logical_or(wall, jnp.logical_and(row == chunk, north))
            flux = face(lower[:5], upper[:5], lower[5], upper[5], wall)
            for f in range(5):
                change[f] = change[f] + (flux[f][1 : chunk + 1] - flux[f][:chunk])
            left = []
            for f in range(5):
                spot = f * depth + z
                left.append(
                    jnp.where(
                        first,
                        pltpu.roll(xrecv[0, rows, :], lax.rem(width - spot, width), 1),
                        pltpu.roll(own[f], 1, 1),
                    )
                )
            flux = face(conserve(left), cons, left[1], own[1], wall_low)
            for f in range(5):
                over = jnp.where(
                    last,
                    pltpu.roll(edge_x[f, rows, :], width - 1 - z, 1),
                    pltpu.roll(flux[f], width - 1, 1),
                )
                change[f] = change[f] + (over - flux[f])
            fresh = [cons[f] - step_ratio * change[f] for f in range(5)]
            scale = inverse(fresh[0])
            out = pl.ds(z * height + y0, chunk)
            adv_ref[0, out, :] = fresh[0]
            for f in range(1, 5):
                adv_ref[f, out, :] = fresh[f] * scale
        plane_out(z).start()
        return carry

    lax.fori_loop(0, depth, plane, 0)

    def pick(s, carry):
        at = [jnp.maximum(map_ref[0, s * cap + r], 0) for r in range(cap)]
        for f in range(5):
            found = [adv_ref[f, pl.ds(b, 1), :] for b in at]
            picked[s, f * cap : (f + 1) * cap, :] = jnp.concatenate(found, 0)
        return carry

    lax.fori_loop(0, n, pick, 0)

    def part(ref, s, j):
        return ref[s, j * cap : (j + 1) * cap, :]

    def couple(ref, s):
        g = part(picked, s, 0)
        scale = 1.0 / (g + part(ref, s, 0))
        fresh = [(g * part(picked, s, 1 + c) + part(ref, s, 1 + c)) * scale for c in range(3)]
        fresh.append((g * part(picked, s, 4) + part(ref, s, 4)) / (g + part(ref, s, 5)))
        for j in range(back):
            new_ref[s, j * cap : (j + 1) * cap, :] = fresh[j]
            adv_ref[1 + j, pl.ds(blocks + s * cap, cap), :] = fresh[j]

    couple(pay_ref, me)
    home[me] = new_ref[me]

    def inward(k):
        d = behind(k)
        return pltpu.make_async_remote_copy(
            src_ref=new_ref.at[d],
            dst_ref=home.at[me],
            send_sem=back_send.at[k],
            recv_sem=back_recv.at[k],
            device_id=place(d),
            device_id_type=MESH,
        )

    def answer(k, carry):
        d = behind(k)
        outward(k).wait()
        couple(got, d)
        inward(k).start()
        return carry

    lax.fori_loop(1, n, answer, 0)

    number = lax.broadcasted_iota(jnp.int32, index_row.shape, 0) * width
    number = number + lax.broadcasted_iota(jnp.int32, index_row.shape, 1)

    def mark(s, index):
        for r in range(cap):
            i = s * cap + r
            index = jnp.where(number == map_ref[0, i], blocks + i, index)
        return index

    index_row[...] = lax.fori_loop(0, n, mark, number)
    index_copy = pltpu.make_async_copy(index_row, index_ref, index_sem)
    index_copy.start()

    index_copy.wait()
    unroll = 8

    def assemble(z, carry):
        def some(i, carry):
            b = z * height + i * unroll
            at = [index_ref[b // width, lax.rem(b, width) + u] for u in range(unroll)]
            for j in range(back):
                found = [adv_ref[1 + j, pl.ds(source, 1), :] for source in at]
                fin_ref[j, pl.ds(b, unroll), :] = jnp.concatenate(found, 0)
            return carry

        lax.fori_loop(0, height // unroll, some, 0)
        final_out(z).start()
        return carry

    lax.fori_loop(0, depth, assemble, 0)

    def finish(k, carry):
        inward(k).wait()
        return carry

    lax.fori_loop(1, n, finish, 0)
    stores[2].start()
    for store in stores:
        store.wait()
    for z in range(depth):
        plane_out(z).wait()
        final_out(z).wait()


def final_kernel(
    cap,
    rank_ref,
    adv_ref,
    ret_hbm,
    calm_hbm,
    pull_hbm,
    out_ref,
    solid_out,
    held,
    ret_ref,
    calm_ref,
    pull_ref,
    solid_ref,
    load_sem,
    store_sem,
):
    slots = rank_ref.shape[0]
    fields, blocks, width = adv_ref.shape
    loads = [
        pltpu.make_async_copy(src, dst, load_sem.at[i])
        for i, (src, dst) in enumerate(
            [(ret_hbm, ret_ref), (calm_hbm, calm_ref), (pull_hbm, pull_ref)]
            + [(adv_ref.at[f], held.at[f]) for f in range(fields)]
        )
    ]
    stores = [
        pltpu.make_async_copy(src, dst, store_sem.at[i])
        for i, (src, dst) in enumerate(
            [(held.at[f], out_ref.at[f]) for f in range(fields)] + [(solid_ref, solid_out)]
        )
    ]
    for load in loads:
        load.start()
    for load in loads[:3]:
        load.wait()
    for f in range(2):
        loads[3 + f].wait()
        stores[f].start()
    unroll = 8

    def solid(i, carry):
        for u in range(unroll):
            k = i * unroll + u
            v = jnp.maximum(rank_ref[k], 0)
            s = v // cap
            r = v % cap
            rows = [ret_ref[s, pl.ds(j * cap + r, 1), :] for j in range(back)]
            for j in range(back):
                solid_ref[j, pl.ds(2 * k, 2), :] = jnp.broadcast_to(rows[j], (2, width))
        return carry

    steps = slots // unroll
    parts = fields - 2
    for p in range(parts):
        lax.fori_loop(p * steps // parts, (p + 1) * steps // parts, solid, 0)
        loads[5 + p].wait()
        stores[2 + p].start()
    for j in range(back):
        solid_ref[j] = calm_ref[j] + pull_ref[j // 3] * solid_ref[j]
    stores[fields].start()
    for store in stores:
        store.wait()


def per_device(
    n_gx,
    n_gy,
    gaseous_rho,
    gaseous_flow_vector,
    gaseous_kelvin,
    sender_tile_map,
    receiver_arrival_rank,
    bin_active_number,
    grain_inertia,
    grain_motion_vector,
    grain_kelvin,
    grain_voxel_number,
    grain_substance_label,
    exchange_factor,
):
    n = n_gx * n_gy
    depth, height, width = gaseous_rho.shape
    slots, padding = grain_inertia.shape
    cap = sender_tile_map.shape[1] // n
    blocks = depth * height
    f32, i32 = jnp.float32, jnp.int32
    shape = jax.ShapeDtypeStruct
    dma = pltpu.SemaphoreType.DMA
    adv, ret, calm, pull = pl.pallas_call(
        functools.partial(grid_kernel, n_gx, n_gy),
        out_shape=(
            shape((5, blocks, width), f32),
            shape((n, back * cap, width), f32),
            shape((back, 2 * slots, width), f32),
            shape((2, 2 * slots, width), f32),
        ),
        in_specs=[ANY] * 12,
        out_specs=(ANY,) * 4,
        scratch_shapes=[
            pltpu.VMEM((5, blocks + n * cap, width), f32),
            pltpu.VMEM((back, blocks, width), f32),
            pltpu.VMEM((blocks // width, width), i32),
            pltpu.SMEM((blocks // width, width), i32),
            pltpu.VMEM((n, back * cap, width), f32),
            pltpu.VMEM((back, 2 * slots, width), f32),
            pltpu.VMEM((2, 2 * slots, width), f32),
            pltpu.VMEM((depth, height, width), f32),
            pltpu.VMEM((3, depth, height, width), f32),
            pltpu.VMEM((depth, height, width), f32),
            pltpu.VMEM((slots, padding), f32),
            pltpu.VMEM((3, slots, padding), f32),
            pltpu.VMEM((slots, padding), f32),
            pltpu.VMEM((slots, padding), i32),
            pltpu.VMEM((slots, padding), i32),
            pltpu.VMEM((1, slots), i32),
            pltpu.SMEM((1, n * cap), i32),
            pltpu.SMEM((1, slots), i32),
            pltpu.SMEM((1, slots), i32),
            pltpu.SMEM((2, 2), f32),
            pltpu.VMEM((sent, slots, width), f32),
            pltpu.VMEM((n, sent * cap, width), f32),
            pltpu.VMEM((2, height, width), f32),
            pltpu.VMEM((2, height, width), f32),
            pltpu.VMEM((2, 5, depth, width), f32),
            pltpu.VMEM((2, 5, depth, width), f32),
            pltpu.VMEM((n, sent * cap, width), f32),
            pltpu.VMEM((n, back * cap, width), f32),
            pltpu.VMEM((6, height + 16, width), f32),
            pltpu.VMEM((5, height, width), f32),
            pltpu.VMEM((5, height, width), f32),
            pltpu.VMEM((n, 5 * cap, width), f32),
            dma((13,)),
            dma((depth,)),
            dma((depth,)),
            dma,
            dma((3,)),
            dma((4,)),
            dma((4,)),
            dma((n,)),
            dma((n,)),
            dma((n,)),
            dma((n,)),
        ],
        compiler_params=pltpu.CompilerParams(
            collective_id=0, has_side_effects=True, vmem_limit_bytes=limit
        ),
        name="advance_and_couple",
    )(
        gaseous_rho,
        gaseous_flow_vector,
        gaseous_kelvin,
        sender_tile_map,
        receiver_arrival_rank.reshape(1, slots),
        bin_active_number.reshape(1, slots),
        grain_inertia,
        grain_motion_vector,
        grain_kelvin,
        grain_voxel_number,
        grain_substance_label,
        exchange_factor,
    )
    final, solid = pl.pallas_call(
        functools.partial(final_kernel, cap),
        out_shape=(shape((5, blocks, width), f32), shape((back, 2 * slots, width), f32)),
        in_specs=[SMEM] + [ANY] * 4,
        out_specs=(ANY, ANY),
        scratch_shapes=[
            pltpu.VMEM((5, blocks, width), f32),
            pltpu.VMEM((n, back * cap, width), f32),
            pltpu.VMEM((back, 2 * slots, width), f32),
            pltpu.VMEM((2, 2 * slots, width), f32),
            pltpu.VMEM((back, 2 * slots, width), f32),
            dma((8,)),
            dma((6,)),
        ],
        compiler_params=pltpu.CompilerParams(vmem_limit_bytes=limit),
        name="place_results",
    )(receiver_arrival_rank, adv, ret, calm, pull)
    return (
        final.reshape(5, depth, height, width),
        solid.reshape(back, slots, 2, width),
    )


def solution(mesh):
    placed = (
        P(None, "gy", "gx"),
        P(None, None, "gy", "gx"),
        P(None, "gy", "gx"),
        P(("gx", "gy"), None),
        P(("gx", "gy")),
        P(("gx", "gy")),
        P(("gx", "gy"), None),
        P(None, ("gx", "gy"), None),
        P(("gx", "gy"), None),
        P(("gx", "gy"), None),
        P(("gx", "gy"), None),
        P(),
    )
    return jax.shard_map(
        functools.partial(per_device, mesh.shape["gx"], mesh.shape["gy"]),
        mesh=mesh,
        in_specs=placed,
        out_specs=(P(None, None, "gy", "gx"), P(None, ("gx", "gy"), None, None)),
        check_vma=False,
    )
```
